256 devices in a mesh: bands: 8 (over z_hi, core), gy: 4 (over x), gz: 8 (over z_lo, y).
Axes of the slice: x: 4, y: 4, z: 8 (z_hi: 4, z_lo: 2; z = z_hi * 2 + z_lo), core: 2. Of those that a mesh axis runs over, the one named last changes fastest.
Arguments:
- orbitals: float32 [16, 64, 128, 128], P('bands', 'gy', 'gz'), may hold values from -6 to 6
- orbital_shift: float32 [16], P('bands'), may hold values from 0.1 to 1
- occupation: float32 [16], P('bands'), may hold values from 0.03125 to 0.125
- potential: float32 [64, 128, 128], P('gy', 'gz'), may hold values from 0.1 to 2
- perturbation: float32 [64, 128, 128], P('gy', 'gz'), may hold values from -6 to 6
- kernel: float32 [64, 128, 128], P('gy', 'gz'), may hold values from 0.2 to 1
Outputs:
- response: float32 [16, 64, 128, 128], P('bands', 'gy', 'gz')
- density: float32 [64, 128, 128], P('gy', 'gz', 'bands')
The draws below stay inside these ranges and needn't reach their ends.
All inputs are finite; a program needn't handle non-finite values.
Results may differ from the reference program's by a relative error of at most 0.00002.
Values sent between devices are 32-bit elements; how exact they have to be, the bound alone decides.
No kernel may reach another device: no remote copies, remote signals or barrier semaphores. Data moves between devices by JAX's collectives and lax.ppermute only.
A program may use at most 64 MiB of HBM per device.

```python
import math
import jax
import jax.numpy as jnp
from jax import lax

NX = 128
SWEEPS = 4
OUTER = 2
ORBS = 16
NY = 64
NZ = 128


def block_scale(key, dims, cuts, low, high):
    level, own = 1.0, jax.random.fold_in(key, 6)
    for axis_at, shards_of in cuts:
        heights = jnp.exp(jax.random.uniform(jax.random.fold_in(own, axis_at), (shards_of,), jnp.float32, low / len(cuts), high / len(cuts)))
        level = level * jnp.repeat(heights, dims[axis_at] // shards_of).reshape([-1 if axis == axis_at else 1 for axis in range(len(dims))])
    return level


def centred(stream_key, extent, scale, limit, shards=(), held_as=jnp.bfloat16):
    gain = block_scale(stream_key, extent, shards, -0.22, 0.18) if shards else 1.0
    array = jax.random.normal(stream_key, extent, jnp.float32) * scale * gain
    return jnp.minimum(jnp.maximum(array, -limit), limit).astype(held_as)


def setup_inputs(seed: int = 0) -> dict:
    splits = jax.random.split(jax.random.key(seed), 7)
    orbitals = centred(splits[0], (ORBS, NY, NZ, NX), 1.0, 6.0, ((0, 8), (1, 4), (2, 8)), jnp.float32)
    orbital_shift = jnp.clip(jnp.exp(math.log(1.0) - 2.3025851 * jax.random.uniform(splits[1], (ORBS,), jnp.float32) ** block_scale(splits[1], (ORBS,), ((0, 8),), -0.2, 0.2)), 0.1, 1.0)
    occupation = jnp.clip(0.03125 + 0.09375 * jax.random.uniform(splits[2], (ORBS,), jnp.float32) ** block_scale(splits[2], (ORBS,), ((0, 8),), -0.2, 0.2), 0.03125, 0.125)
    potential = jnp.clip(jnp.exp(math.log(2.0) - 2.9957323 * jax.random.uniform(splits[3], (NY, NZ, NX), jnp.float32) ** block_scale(splits[3], (NY, NZ, NX), ((0, 4), (1, 8)), -0.2, 0.2)), 0.1, 2.0)
    perturbation = centred(splits[4], (NY, NZ, NX), 1.0, 6.0, ((0, 4), (1, 8)), jnp.float32)
    kernel = jnp.clip(0.2 + 0.8 * jax.random.uniform(splits[5], (NY, NZ, NX), jnp.float32) ** block_scale(splits[5], (NY, NZ, NX), ((0, 4), (1, 8)), -0.2, 0.2), 0.2, 1.0)
    return dict(orbitals=orbitals, orbital_shift=orbital_shift, occupation=occupation, potential=potential, perturbation=perturbation, kernel=kernel)


relax_factor = 0.8


def roll_sum(field):
    return jnp.roll(field, 1, -1) + jnp.roll(field, -1, -1)


def laplace_parts(padded):
    centre = padded[..., 1:-1, 1:-1, :]
    along_y = padded[..., 2:, 1:-1, :] + padded[..., :-2, 1:-1, :]
    along_z = padded[..., 1:-1, 2:, :] + padded[..., 1:-1, :-2, :]
    plane_corners = padded[..., 2:, 2:, :] + padded[..., 2:, :-2, :] + padded[..., :-2, 2:, :] + padded[..., :-2, :-2, :]
    face_sum = roll_sum(centre) + along_y + along_z
    edge_sum = roll_sum(along_y) + roll_sum(along_z) + plane_corners
    corner_sum = roll_sum(plane_corners)
    laplacian = (-128.0 * centre + 14.0 * face_sum + 3.0 * edge_sum + corner_sum) / 30.0
    return centre, laplacian


def mehrstellen(padded):
    centre = padded[..., 1:-1, 1:-1, :]
    along_y = padded[..., 2:, 1:-1, :] + padded[..., :-2, 1:-1, :]
    along_z = padded[..., 1:-1, 2:, :] + padded[..., 1:-1, :-2, :]
    return 0.5 * centre + (roll_sum(centre) + along_y + along_z) / 12.0


def relax(padded, weight, source):
    centre, laplacian = laplace_parts(padded)
    diagonal = 32.0 / 15.0 + weight
    applied = -0.5 * laplacian + weight * centre
    return centre + relax_factor * (source - applied) / diagonal


def wrapped(field):
    return jnp.pad(field, ((1, 1), (1, 1), (0, 0)), mode="wrap")


def reference(orbitals, orbital_shift, occupation, potential, perturbation, kernel):
    change = perturbation
    response = jnp.zeros_like(orbitals)
    density = jnp.zeros_like(potential)
    for update in range(OUTER):
        def relax_orbital(accumulated, element):
            orbital, shift_value, weight_value, field = element
            weight = potential + shift_value
            source = -mehrstellen(wrapped(change * orbital))
            for sweep_index in range(SWEEPS):
                field = relax(wrapped(field), weight, source)
            return accumulated + weight_value * orbital * field, field

        density, response = lax.scan(relax_orbital, jnp.zeros_like(potential), (orbitals, orbital_shift, occupation, response))
        if update + 1 < OUTER:
            change = perturbation + kernel * density
    return response, density
```

```python
import jax
import jax.numpy as jnp
from jax import lax
from jax.experimental import pallas as pl
from jax.experimental.pallas import tpu as pltpu
from jax.sharding import PartitionSpec as P

RELAX = 0.8
HALO = 4
VMEM = pl.BlockSpec(memory_space=pltpu.VMEM)
SMEM = pl.BlockSpec(memory_space=pltpu.SMEM)


def call(body, outs, *args, scratch=(), smem=0):
    return pl.pallas_call(
        body,
        out_shape=outs,
        in_specs=[VMEM] * (len(args) - smem) + [SMEM] * smem,
        out_specs=jax.tree.map(lambda _: VMEM, outs),
        scratch_shapes=list(scratch),
        compiler_params=pltpu.CompilerParams(vmem_limit_bytes=48 * 2**20),
    )(*args)


def f32(*shape):
    return jax.ShapeDtypeStruct(shape, jnp.float32)


def low_half():
    return lax.broadcasted_iota(jnp.int32, (8, 128), 0) < 4


def pack_z(row, head_ref, tail_ref, field):
    low = low_half()
    for j in range(12):
        a, b = row(j), row(j + 12)
        head_ref[field, j] = jnp.where(low, a[:8], pltpu.roll(b[:8], 4, 0))
        tail_ref[field, j] = jnp.where(low, pltpu.roll(b[8:], 4, 0), a[8:])


def padded_row(centre_ref, lo_ref, hi_ref, field):
    def row(r):
        if r < 4:
            return lo_ref[field, r]
        if r < 20:
            return centre_ref[field, r - 4]
        return hi_ref[field, r - 20]

    return row


def pack_kernel(centre_ref, lo_ref, hi_ref, head_ref, tail_ref):
    for field in range(centre_ref.shape[0]):
        pack_z(padded_row(centre_ref, lo_ref, hi_ref, field), head_ref, tail_ref, field)


def assemble(row, above_ref, below_ref, field, dest_ref, at):
    low = low_half()
    for r in range(24):
        dest_ref[at, r, 0:16] = row(r)
    for j in range(12):
        above, below = above_ref[field, j], below_ref[field, j]
        dest_ref[at, j, 16:24] = jnp.where(low, above, below)
        dest_ref[at, j + 12, 16:24] = pltpu.roll(jnp.where(low, below, above), 4, 0)


def shifts_z(u):
    return pltpu.roll(u, 1, u.ndim - 2) + pltpu.roll(u, 23, u.ndim - 2)


def shifts_x(u):
    return pltpu.roll(u, 1, u.ndim - 1) + pltpu.roll(u, 127, u.ndim - 1)


def by_rows(first, last, load, emit, step=2):
    def body(i, carry):
        before, at = carry
        r = first + step * i
        for k in range(step):
            after = load(r + k + 1)
            emit(r + k, before, at, after)
            before, at = at, after
        return before, at

    lax.fori_loop(0, (last - first) // step, body, (load(first - 1), load(first)))


def sources(p_ref, scale_ref, sc_ref, o):
    def load(r):
        return p_ref[o, r]

    def emit(r, before, at, after):
        faces = shifts_x(at) + shifts_z(at) + (before + after)
        sc_ref[o, r] = scale_ref[o, r] * (-30.0 * at - 5.0 * faces)

    by_rows(1, 23, load, emit)


def sweep(src_ref, scale_ref, sc_ref, o, margin, store):
    def load(r):
        u = src_ref[o, r]
        return u, shifts_z(u)

    def emit(r, before, at, after):
        u, along_z = at
        across = before[1] + after[1]
        m = before[0] + after[0] + along_z
        n = 3.0 * m + across
        total = shifts_x(14.0 * u + n) + (3.0 * n + 5.0 * m)
        store(r, 0.2 * u + sc_ref[o, r] + scale_ref[o, r] * total)

    by_rows(margin, 24 - margin, load, emit)


def into(dest_ref, o):
    def store(r, new):
        dest_ref[o, r] = new

    return store


def last_sweep(src_ref, scale_ref, sc_ref, o, orb_ref, occ_ref, resp_ref, dens_ref):
    occupation = occ_ref[o]

    def store(r, new):
        own = new[:16]
        resp_ref[o, r - 4] = own
        term = occupation * orb_ref[o, r - 4] * own
        dens_ref[r - 4] = term if o == 0 else dens_ref[r - 4] + term

    sweep(src_ref, scale_ref, sc_ref, o, 4, store)


def first_kernel(
    centre_ref, lo_ref, hi_ref, above_ref, below_ref, orb_ref, shift_ref, occ_ref,
    resp_ref, dens_ref, scale_ref, p_ref, sc_ref, a_ref, b_ref,
):
    for field in range(2):
        assemble(padded_row(centre_ref, lo_ref, hi_ref, field), above_ref, below_ref, field, p_ref, field)
    assemble(padded_row(centre_ref, lo_ref, hi_ref, 2), above_ref, below_ref, 2, a_ref, 0)
    for o in range(2):
        base = 32.0 / 15.0 + shift_ref[o]

        def scales(r, _):
            scale_ref[o, r] = (RELAX / 60.0) / (base + a_ref[0, r])
            return 0

        lax.fori_loop(1, 23, scales, 0)
    for o in range(2):
        sources(p_ref, scale_ref, sc_ref, o)
    for o in range(2):
        sweep(sc_ref, scale_ref, sc_ref, o, 2, into(a_ref, o))
        sweep(a_ref, scale_ref, sc_ref, o, 3, into(b_ref, o))
        last_sweep(b_ref, scale_ref, sc_ref, o, orb_ref, occ_ref, resp_ref, dens_ref)


def change_kernel(own_ref, other_ref, pert_ref, kern_ref, orb_ref, resp_ref, core_ref, centre_ref, up_ref, down_ref):
    first_core = core_ref[0] == 0
    for y in range(16):
        mine, theirs = own_ref[y % 8], other_ref[y % 8]
        total = jnp.where(first_core, mine, theirs) if y < 8 else jnp.where(first_core, theirs, mine)
        change = pert_ref[y] + kern_ref[y] * total
        for o in range(2):
            product, response = change * orb_ref[o, y], resp_ref[o, y]
            centre_ref[o, y] = product
            centre_ref[2 + o, y] = response
            if y < 4:
                down_ref[o, y] = product
                down_ref[2 + o, y] = response
            if y >= 12:
                up_ref[o, y - 12] = product
                up_ref[2 + o, y - 12] = response


def swap_blocks(rows):
    block = lax.broadcasted_iota(jnp.int32, rows[0].shape, rows[0].ndim - 1) // 16
    for d in (1, 2, 4):
        keep = (block // d) % 2 == 0
        out = list(rows)
        for k in range(8):
            if k & d == 0:
                a, b = rows[k], rows[k + d]
                out[k] = jnp.where(keep, a, pltpu.roll(b, 16 * d, 1))
                out[k + d] = jnp.where(keep, pltpu.roll(a, 128 - 16 * d, 1), b)
        rows = out
    return rows


def second_kernel(
    centre_ref, lo_ref, hi_ref, above_ref, below_ref, scale_ref, orb_ref, occ_ref,
    resp_ref, out_ref, p_ref, u_ref, sc_ref, a_ref, b_ref, dens_ref,
):
    for o in range(2):
        assemble(padded_row(centre_ref, lo_ref, hi_ref, o), above_ref, below_ref, o, p_ref, o)
        assemble(padded_row(centre_ref, lo_ref, hi_ref, 2 + o), above_ref, below_ref, 2 + o, u_ref, o)
    for o in range(2):
        sources(p_ref, scale_ref, sc_ref, o)
        sweep(u_ref, scale_ref, sc_ref, o, 1, into(a_ref, o))
        sweep(a_ref, scale_ref, sc_ref, o, 2, into(b_ref, o))
        sweep(b_ref, scale_ref, sc_ref, o, 3, into(a_ref, o))
        last_sweep(a_ref, scale_ref, sc_ref, o, orb_ref, occ_ref, resp_ref, dens_ref)
    for part in range(4):
        y, z = part // 2, 8 * (part % 2)
        blocks = swap_blocks([dens_ref[2 * k + y, z : z + 8] for k in range(8)])
        for b in range(8):
            out_ref[b, part] = blocks[b]


def final_kernel(own_ref, one_ref, two_ref, three_ref, dens_ref):
    for part in range(4):
        y, z = part // 2, 8 * (part % 2)
        total = (own_ref[part] + one_ref[part]) + (two_ref[part] + three_ref[part])
        for k in range(8):
            moved = total if k == 0 else pltpu.roll(total, 128 - 16 * k, 1)
            dens_ref[2 * k + y, z : z + 8, :] = moved[:, :16]


def ring(axis, step):
    count = lax.axis_size(axis)
    return [(i, (i + step) % count) for i in range(count)]


def exchange_y(up, down):
    return lax.ppermute(up, "gy", ring("gy", 1)), lax.ppermute(down, "gy", ring("gy", -1))


def exchange_z(centre, lo, hi):
    fields = centre.shape[0]
    strip = f32(fields, 12, 8, 128)
    head, tail = call(pack_kernel, (strip, strip), centre, lo, hi)
    above = lax.ppermute(head, "gz", ring("gz", -1))
    below = lax.ppermute(tail, "gz", ring("gz", 1))
    return above, below


def partner(value, step):
    count = lax.axis_size("bands")
    return lax.ppermute(value, "bands", [(i, i ^ step) for i in range(count)])


def on_device(orbitals, orbital_shift, occupation, potential, perturbation, kernel):
    group = lax.axis_index("bands")
    core, far = group % 2, group // 2
    padded = f32(2, 24, 24, 128)
    wide = pltpu.VMEM((2, 24, 24, 128), jnp.float32)

    def fields(rows):
        return jnp.concatenate([perturbation[None, rows] * orbitals[:, rows], potential[None, rows]], 0)

    lo, hi = exchange_y(fields(slice(12, 16)), fields(slice(0, 4)))
    centre = fields(slice(0, 16))
    above, below = exchange_z(centre, lo, hi)
    response, partial, scale = call(
        first_kernel, (f32(2, 16, 16, 128), f32(16, 16, 128), padded),
        centre, lo, hi, above, below, orbitals, orbital_shift, occupation,
        scratch=[wide] * 4, smem=2,
    )

    own = lax.dynamic_slice_in_dim(partial, 8 * core, 8, 0)
    own = own + partner(lax.dynamic_slice_in_dim(partial, 8 * (1 - core), 8, 0), 1)
    own = own + partner(own, 2)
    own = own + partner(own, 6)
    other = partner(own, 1)
    centre, up, down = call(
        change_kernel, (f32(4, 16, 16, 128), f32(4, 4, 16, 128), f32(4, 4, 16, 128)),
        own, other, perturbation, kernel, orbitals, response, core[None].astype(jnp.int32), smem=1,
    )
    lo, hi = exchange_y(up, down)
    above, below = exchange_z(centre, lo, hi)
    response, blocks = call(
        second_kernel, (f32(2, 16, 16, 128), f32(8, 4, 8, 128)),
        centre, lo, hi, above, below, scale, orbitals, occupation,
        scratch=[wide] * 5 + [pltpu.VMEM((16, 16, 128), jnp.float32)], smem=1,
    )

    blocks = blocks.reshape(4, 2, 4, 8, 128)
    kept = lax.dynamic_index_in_dim(blocks, core, 1, keepdims=False)
    kept = kept + partner(lax.dynamic_index_in_dim(blocks, 1 - core, 1, keepdims=False), 1)

    def block_of(step):
        return lax.dynamic_index_in_dim(kept, far ^ step, 0, keepdims=False)

    two, one, three = (partner(block_of(step), 2 * step) for step in (2, 1, 3))
    density = call(final_kernel, f32(16, 16, 16), block_of(0), one, two, three)
    return response, density


def solution(mesh):
    placed = (
        P("bands", "gy", "gz", None),
        P("bands"),
        P("bands"),
        P("gy", "gz", None),
        P("gy", "gz", None),
        P("gy", "gz", None),
    )
    return jax.shard_map(
        on_device,
        mesh=mesh,
        in_specs=placed,
        out_specs=(P("bands", "gy", "gz", None), P("gy", "gz", "bands")),
        check_vma=False,
    )
```

```python
import jax
import jax.numpy as jnp
from jax import lax
from jax.experimental import pallas as pl
from jax.experimental.pallas import tpu as pltpu
from jax.sharding import PartitionSpec as P

RELAX = 0.8
HALO = 4
VMEM = pl.BlockSpec(memory_space=pltpu.VMEM)
SMEM = pl.BlockSpec(memory_space=pltpu.SMEM)


def call(body, outs, *args, scratch=(), smem=0, where=VMEM):
    return pl.pallas_call(
        body,
        out_shape=outs,
        in_specs=[where] * (len(args) - smem) + [SMEM] * smem,
        out_specs=jax.tree.map(lambda _: VMEM, outs),
        scratch_shapes=list(scratch),
        compiler_params=pltpu.CompilerParams(vmem_limit_bytes=48 * 2**20),
    )(*args)


def f32(*shape):
    return jax.ShapeDtypeStruct(shape, jnp.float32)


def low_half():
    return lax.broadcasted_iota(jnp.int32, (8, 128), 0) < 4


def pack_z(row, even, near_ref, far_ref, field):
    low = low_half()
    for j in range(12):
        a, b = row(j), row(j + 12)
        head = jnp.where(low, a[:8], pltpu.roll(b[:8], 4, 0))
        tail = jnp.where(low, pltpu.roll(b[8:], 4, 0), a[8:])
        near_ref[field, j] = jnp.where(even, tail, head)
        far_ref[field, j] = jnp.where(even, head, tail)


def padded_row(centre_ref, lo_ref, hi_ref, field):
    def row(r):
        if r < 4:
            return lo_ref[field, r]
        if r < 20:
            return centre_ref[field, r - 4]
        return hi_ref[field, r - 20]

    return row


def pack_kernel(centre_ref, lo_ref, hi_ref, odd_ref, far_ref, near_ref):
    even = odd_ref[0] == 0
    for field in range(centre_ref.shape[0]):
        pack_z(padded_row(centre_ref, lo_ref, hi_ref, field), even, near_ref, far_ref, field)


def assemble(row, near_ref, far_ref, field, odd_ref, dest_ref, at):
    low, even = low_half(), odd_ref[0] == 0
    for r in range(24):
        dest_ref[at, r, 0:16] = row(r)
    for j in range(12):
        near, far = near_ref[field, j], far_ref[field, j]
        above, below = jnp.where(even, near, far), jnp.where(even, far, near)
        dest_ref[at, j, 16:24] = jnp.where(low, above, below)
        dest_ref[at, j + 12, 16:24] = pltpu.roll(jnp.where(low, below, above), 4, 0)


def shifts_z(u):
    return pltpu.roll(u, 1, u.ndim - 2) + pltpu.roll(u, 23, u.ndim - 2)


def shifts_x(u):
    return pltpu.roll(u, 1, u.ndim - 1) + pltpu.roll(u, 127, u.ndim - 1)


def by_rows(first, last, load, emit):
    before, at = load(first - 1), load(first)
    for r in range(first, last):
        after = load(r + 1)
        emit(r, before, at, after)
        before, at = at, after


def sources(p_ref, scale_ref, sc_ref, o):
    def load(r):
        return p_ref[o, r]

    def emit(r, before, at, after):
        faces = shifts_x(at) + shifts_z(at) + (before + after)
        sc_ref[o, r] = scale_ref[o, r] * (-30.0 * at - 5.0 * faces)

    by_rows(1, 23, load, emit)


def sweep(src_ref, scale_ref, sc_ref, o, margin, store):
    def load(r):
        u = src_ref[o, r]
        return u, shifts_z(u)

    def emit(r, before, at, after):
        u, along_z = at
        across = before[1] + after[1]
        m = before[0] + after[0] + along_z
        n = 3.0 * m + across
        total = shifts_x(14.0 * u + n) + (3.0 * n + 5.0 * m)
        store(r, 0.2 * u + sc_ref[o, r] + scale_ref[o, r] * total)

    by_rows(margin, 24 - margin, load, emit)


def into(dest_ref, o):
    def store(r, new):
        dest_ref[o, r] = new

    return store


def last_sweep(src_ref, scale_ref, sc_ref, o, orb_ref, occ_ref, resp_ref, dens_ref):
    occupation = occ_ref[o]

    def store(r, new):
        own = new[:16]
        resp_ref[o, r - 4] = own
        term = occupation * orb_ref[o, r - 4] * own
        dens_ref[r - 4] = term if o == 0 else dens_ref[r - 4] + term

    sweep(src_ref, scale_ref, sc_ref, o, 4, store)


def first_kernel(
    centre_ref, lo_ref, hi_ref, far_ref, near_ref, orb_ref, shift_ref, occ_ref, odd_ref,
    resp_ref, dens_ref, scale_ref, p_ref, sc_ref, a_ref, b_ref,
):
    for field in range(2):
        assemble(padded_row(centre_ref, lo_ref, hi_ref, field), near_ref, far_ref, field, odd_ref, p_ref, field)
    assemble(padded_row(centre_ref, lo_ref, hi_ref, 2), near_ref, far_ref, 2, odd_ref, a_ref, 0)
    for o in range(2):
        base = 32.0 / 15.0 + shift_ref[o]

        for r in range(1, 23):
            scale_ref[o, r] = (RELAX / 60.0) / (base + a_ref[0, r])
    for o in range(2):
        sources(p_ref, scale_ref, sc_ref, o)
    for o in range(2):
        sweep(sc_ref, scale_ref, sc_ref, o, 2, into(a_ref, o))
        sweep(a_ref, scale_ref, sc_ref, o, 3, into(b_ref, o))
        last_sweep(b_ref, scale_ref, sc_ref, o, orb_ref, occ_ref, resp_ref, dens_ref)


def product_kernel(orb_hbm, pert_hbm, pot_hbm, centre_ref, up_ref, down_ref, orb_ref, pert_ref, pot_ref, sems):
    pairs = ((orb_hbm, orb_ref), (pert_hbm, pert_ref), (pot_hbm, pot_ref))
    copies = [pltpu.make_async_copy(src, dest, sems.at[i]) for i, (src, dest) in enumerate(pairs)]
    for copy in copies:
        copy.start()
    for copy in copies:
        copy.wait()
    for y in range(16):
        for field in range(3):
            value = pot_ref[y] if field == 2 else pert_ref[y] * orb_ref[field, y]
            centre_ref[field, y] = value
            if y < 4:
                down_ref[field, y] = value
            if y >= 12:
                up_ref[field, y - 12] = value


def change_kernel(own_ref, other_ref, pert_ref, kern_ref, orb_ref, resp_ref, core_ref, centre_ref, up_ref, down_ref):
    first_core = core_ref[0] == 0
    for y in range(16):
        mine, theirs = own_ref[y % 8], other_ref[y % 8]
        total = jnp.where(first_core, mine, theirs) if y < 8 else jnp.where(first_core, theirs, mine)
        change = pert_ref[y] + kern_ref[y] * total
        for o in range(2):
            product, response = change * orb_ref[o, y], resp_ref[o, y]
            centre_ref[o, y] = product
            centre_ref[2 + o, y] = response
            if y < 4:
                down_ref[o, y] = product
                down_ref[2 + o, y] = response
            if y >= 12:
                up_ref[o, y - 12] = product
                up_ref[2 + o, y - 12] = response


def swap_blocks(rows):
    block = lax.broadcasted_iota(jnp.int32, rows[0].shape, rows[0].ndim - 1) // 16
    for d in (1, 2, 4):
        keep = (block // d) % 2 == 0
        out = list(rows)
        for k in range(8):
            if k & d == 0:
                a, b = rows[k], rows[k + d]
                out[k] = jnp.where(keep, a, pltpu.roll(b, 16 * d, 1))
                out[k + d] = jnp.where(keep, pltpu.roll(a, 128 - 16 * d, 1), b)
        rows = out
    return rows


def second_kernel(
    centre_ref, lo_ref, hi_ref, far_ref, near_ref, scale_ref, orb_ref, occ_ref, odd_ref,
    resp_ref, out_ref, p_ref, u_ref, sc_ref, a_ref, b_ref, dens_ref,
):
    for o in range(2):
        assemble(padded_row(centre_ref, lo_ref, hi_ref, o), near_ref, far_ref, o, odd_ref, p_ref, o)
        assemble(padded_row(centre_ref, lo_ref, hi_ref, 2 + o), near_ref, far_ref, 2 + o, odd_ref, u_ref, o)
    for o in range(2):
        sources(p_ref, scale_ref, sc_ref, o)
        sweep(u_ref, scale_ref, sc_ref, o, 1, into(a_ref, o))
        sweep(a_ref, scale_ref, sc_ref, o, 2, into(b_ref, o))
        sweep(b_ref, scale_ref, sc_ref, o, 3, into(a_ref, o))
        last_sweep(a_ref, scale_ref, sc_ref, o, orb_ref, occ_ref, resp_ref, dens_ref)
    for part in range(4):
        y, z = part // 2, 8 * (part % 2)
        blocks = swap_blocks([dens_ref[2 * k + y, z : z + 8] for k in range(8)])
        for b in range(8):
            out_ref[b, part] = blocks[b]


def final_kernel(own_ref, one_ref, two_ref, three_ref, dens_ref):
    for part in range(4):
        y, z = part // 2, 8 * (part % 2)
        total = (own_ref[part] + one_ref[part]) + (two_ref[part] + three_ref[part])
        for k in range(8):
            moved = total if k == 0 else pltpu.roll(total, 128 - 16 * k, 1)
            dens_ref[2 * k + y, z : z + 8, :] = moved[:, :16]


def ring(axis, step):
    count = lax.axis_size(axis)
    return [(i, (i + step) % count) for i in range(count)]


def exchange_y(up, down):
    return lax.ppermute(up, "gy", ring("gy", 1)), lax.ppermute(down, "gy", ring("gy", -1))


def exchange_z(centre, lo, hi, odd):
    fields = centre.shape[0]
    strip = f32(fields, 12, 8, 128)
    far, near = call(pack_kernel, (strip, strip), centre, lo, hi, odd, smem=1)
    count = lax.axis_size("gz")
    far = lax.ppermute(far, "gz", far_pairs(count))
    near = lax.ppermute(near, "gz", [(i, i ^ 1) for i in range(count)])
    return near, far


def far_pairs(count):
    return [(i, (i - 1) % count if i % 2 == 0 else (i + 1) % count) for i in range(count)]


def partner(value, step):
    count = lax.axis_size("bands")
    return lax.ppermute(value, "bands", [(i, i ^ step) for i in range(count)])


def on_device(orbitals, orbital_shift, occupation, potential, perturbation, kernel):
    group = lax.axis_index("bands")
    core, chip = group % 2, group // 2
    padded = f32(2, 24, 24, 128)
    wide = pltpu.VMEM((2, 24, 24, 128), jnp.float32)

    odd = (lax.axis_index("gz") % 2)[None].astype(jnp.int32)
    centre, up, down = call(
        product_kernel, (f32(3, 16, 16, 128), f32(3, 4, 16, 128), f32(3, 4, 16, 128)),
        orbitals, perturbation, potential, where=pl.BlockSpec(memory_space=pltpu.HBM),
        scratch=[pltpu.VMEM(shape, jnp.float32) for shape in ((2, 16, 16, 128), (16, 16, 128), (16, 16, 128))]
        + [pltpu.SemaphoreType.DMA((3,))],
    )
    lo, hi = exchange_y(up, down)
    near, far = exchange_z(centre, lo, hi, odd)
    response, partial, scale = call(
        first_kernel, (f32(2, 16, 16, 128), f32(16, 16, 128), padded),
        centre, lo, hi, far, near, orbitals, orbital_shift, occupation, odd,
        scratch=[wide] * 4, smem=3,
    )

    own = lax.dynamic_slice_in_dim(partial, 8 * core, 8, 0)
    own = own + partner(lax.dynamic_slice_in_dim(partial, 8 * (1 - core), 8, 0), 1)
    own = own + partner(own, 2)
    own = own + partner(own, 6)
    other = partner(own, 1)
    centre, up, down = call(
        change_kernel, (f32(4, 16, 16, 128), f32(4, 4, 16, 128), f32(4, 4, 16, 128)),
        own, other, perturbation, kernel, orbitals, response, core[None].astype(jnp.int32), smem=1,
    )
    lo, hi = exchange_y(up, down)
    near, far = exchange_z(centre, lo, hi, odd)
    response, blocks = call(
        second_kernel, (f32(2, 16, 16, 128), f32(8, 4, 8, 128)),
        centre, lo, hi, far, near, scale, orbitals, occupation, odd,
        scratch=[wide] * 5 + [pltpu.VMEM((16, 16, 128), jnp.float32)], smem=2,
    )

    blocks = blocks.reshape(4, 2, 4, 8, 128)
    kept = lax.dynamic_index_in_dim(blocks, core, 1, keepdims=False)
    kept = kept + partner(lax.dynamic_index_in_dim(blocks, 1 - core, 1, keepdims=False), 1)

    def block_of(step):
        return lax.dynamic_index_in_dim(kept, chip ^ step, 0, keepdims=False)

    two, one, three = (partner(block_of(step), 2 * step) for step in (2, 1, 3))
    density = call(final_kernel, f32(16, 16, 16), block_of(0), one, two, three)
    return response, density


def solution(mesh):
    placed = (
        P("bands", "gy", "gz", None),
        P("bands"),
        P("bands"),
        P("gy", "gz", None),
        P("gy", "gz", None),
        P("gy", "gz", None),
    )
    return jax.shard_map(
        on_device,
        mesh=mesh,
        in_specs=placed,
        out_specs=(P("bands", "gy", "gz", None), P("gy", "gz", "bands")),
        check_vma=False,
    )
```

```python
import jax
import jax.numpy as jnp
from jax import lax
from jax.experimental import pallas as pl
from jax.experimental.pallas import tpu as pltpu
from jax.sharding import PartitionSpec as P

RELAX = 0.8
VMEM = pl.BlockSpec(memory_space=pltpu.VMEM)
SMEM = pl.BlockSpec(memory_space=pltpu.SMEM)
HBM = pl.BlockSpec(memory_space=pltpu.HBM)

Y_ROWS = 35
Z_TILES = 130


def call(body, outs, *args, scratch=(), smem=0, where=VMEM, limit=16 * 2**20):
    return pl.pallas_call(
        body,
        out_shape=outs,
        in_specs=[where] * (len(args) - smem) + [SMEM] * smem,
        out_specs=jax.tree.map(lambda _: VMEM, outs),
        scratch_shapes=list(scratch),
        compiler_params=pltpu.CompilerParams(vmem_limit_bytes=limit),
    )(*args)


def f32(*shape):
    return jax.ShapeDtypeStruct(shape, jnp.float32)


def scratch32(*shape):
    return pltpu.VMEM(shape, jnp.float32)


def low_half():
    return lax.broadcasted_iota(jnp.int32, (8, 128), 0) < 4


def strip_row(kind, o, tail_of, y):
    base, width = {"product": (8 * o, 8), "potential": (16, 7), "orbital": (23 + 4 * o, 4), "kernel": (31, 4)}[kind]
    return base + (y + width if tail_of else y - 16)


def border_rows():
    for o in range(2):
        for i in range(8):
            yield "product", o, i, 8 + i
    for i in range(7):
        yield "potential", 0, i, 9 + i
    for o in range(2):
        for i in range(4):
            yield "orbital", o, i, 12 + i
    for i in range(4):
        yield "kernel", 0, i, 12 + i


def own_row(refs, kind, o, y):
    orb_ref, pert_ref, pot_ref, kern_ref = refs
    if kind == "product":
        return pert_ref[y] * orb_ref[o, y]
    if kind == "potential":
        return pot_ref[y]
    return orb_ref[o, y] if kind == "orbital" else kern_ref[y]


def strips_kernel(orb_hbm, pert_hbm, pot_hbm, kern_hbm, place_ref, near_ref, far_ref, orb_ref, pert_ref, pot_ref, kern_ref, sems):
    refs = (orb_ref, pert_ref, pot_ref, kern_ref)
    copies = [
        pltpu.make_async_copy(src, dest, sems.at[i])
        for i, (src, dest) in enumerate(zip((orb_hbm, pert_hbm, pot_hbm, kern_hbm), refs))
    ]
    for copy in copies:
        copy.start()
    for copy in copies:
        copy.wait()
    even = place_ref[0] == 0
    for at, (kind, o, head_y, tail_y) in enumerate(border_rows()):
        head, tail = own_row(refs, kind, o, head_y), own_row(refs, kind, o, tail_y)
        near_ref[at] = jnp.where(even, tail, head)
        far_ref[at] = jnp.where(even, head, tail)


def row_reader(refs, near_ref, far_ref, place_ref):
    even = place_ref[0] == 0

    def row(kind, o, y):
        if y < 0:
            at = strip_row(kind, o, True, y)
            return jnp.where(even, far_ref[at], near_ref[at])
        if y >= 16:
            at = strip_row(kind, o, False, y)
            return jnp.where(even, near_ref[at], far_ref[at])
        return own_row(refs, kind, o, y)

    return row


def wide_fields():
    return ("product", 0, 0, -8), ("product", 1, 32, -8), ("potential", 0, 64, -7)


def narrow_fields():
    return ("orbital", 0, 94), ("orbital", 1, 106), ("kernel", 0, 118)


def pack_kernel(orb_ref, pert_ref, pot_ref, kern_ref, ynear_ref, yfar_ref, place_ref, far_ref, near_ref):
    row = row_reader((orb_ref, pert_ref, pot_ref, kern_ref), ynear_ref, yfar_ref, place_ref)
    even, low = place_ref[1] == 0, low_half()

    def put(at, head, tail):
        near_ref[at] = jnp.where(even, tail, head)
        far_ref[at] = jnp.where(even, head, tail)

    for kind, o, at, first in wide_fields():
        for y in range(first, 16 - first):
            cells = row(kind, o, y)
            put(at + y - first, cells[:8], cells[8:])
    for kind, o, at in narrow_fields():
        for j in range(12):
            a, b = row(kind, o, j - 4), row(kind, o, j + 8)
            head = jnp.where(low, a[:8], pltpu.roll(b[:8], 4, 0))
            tail = jnp.where(low, pltpu.roll(b[8:], 4, 0), a[8:])
            put(at + j, head, tail)


def shifts_z(u):
    return pltpu.roll(u, 1, u.ndim - 2) + pltpu.roll(u, u.shape[-2] - 1, u.ndim - 2)


def shifts_x(u):
    return pltpu.roll(u, 1, u.ndim - 1) + pltpu.roll(u, 127, u.ndim - 1)


def by_rows(first, last, load, emit):
    before, at = load(first - 1), load(first)
    for r in range(first, last):
        after = load(r + 1)
        emit(r, before, at, after)
        before, at = at, after


def sources(p_ref, scale_ref, sc_ref, o):
    def load(r):
        return p_ref[o, r]

    def emit(r, before, at, after):
        faces = shifts_x(at) + shifts_z(at) + (before + after)
        sc_ref[o, r] = scale_ref[o, r] * (-30.0 * at - 5.0 * faces)

    by_rows(1, p_ref.shape[1] - 1, load, emit)


def sweep(src_ref, scale_ref, sc_ref, o, margin, store):
    def load(r):
        u = src_ref[o, r]
        return u, shifts_z(u)

    def emit(r, before, at, after):
        u, along_z = at
        across = before[1] + after[1]
        m = before[0] + after[0] + along_z
        n = 3.0 * m + across
        total = shifts_x(14.0 * u + n) + (3.0 * n + 5.0 * m)
        store(r, 0.2 * u + sc_ref[o, r] + scale_ref[o, r] * total)

    by_rows(margin, src_ref.shape[1] - margin, load, emit)


def into(dest_ref, o):
    def store(r, new):
        dest_ref[o, r] = new

    return store


def first_kernel(
    orb_ref, pert_ref, pot_ref, kern_ref, ynear_ref, yfar_ref, zfar_ref, znear_ref, shift_ref, occ_ref, place_ref,
    resp_ref, dens_ref, scale_ref, prod_ref, orbs_ref, kerns_ref, p_ref, s_ref, sc_ref, a_ref, b_ref, pot_scr,
):
    row = row_reader((orb_ref, pert_ref, pot_ref, kern_ref), ynear_ref, yfar_ref, place_ref)
    even, low = place_ref[1] == 0, low_half()

    def sides(at):
        near, far = znear_ref[at], zfar_ref[at]
        return jnp.where(even, near, far), jnp.where(even, far, near)

    for kind, o, at, first in wide_fields():
        dest = pot_scr if kind == "potential" else p_ref.at[o]
        for y in range(first, 16 - first):
            above, below = sides(at + y - first)
            dest[y + 8, 0:16] = row(kind, o, y)
            dest[y + 8, 16:24] = above
            dest[y + 8, 24:32] = below
    for kind, o, at in narrow_fields():
        dest = kerns_ref if kind == "kernel" else orbs_ref.at[o]
        for r in range(24):
            dest[r, 0:16] = row(kind, o, r - 4)
        for j in range(12):
            above, below = sides(at + j)
            dest[j, 16:24] = jnp.where(low, above, below)
            dest[j + 12, 16:24] = pltpu.roll(jnp.where(low, below, above), 4, 0)

    def narrow(dest, r, cells):
        dest[r, 0:16] = cells[:16]
        dest[r, 16:24] = jnp.where(low, cells[16:24], cells[24:32])

    for o in range(2):
        base = 32.0 / 15.0 + shift_ref[o]
        for r in range(1, 31):
            scale = (RELAX / 60.0) / (base + pot_scr[r])
            s_ref[o, r] = scale
            if 4 <= r < 28:
                narrow(scale_ref.at[o], r - 4, scale)
                narrow(prod_ref.at[o], r - 4, p_ref[o, r])
        sources(p_ref, s_ref, sc_ref, o)
        sweep(sc_ref, s_ref, sc_ref, o, 2, into(a_ref, o))
        sweep(a_ref, s_ref, sc_ref, o, 3, into(b_ref, o))
        occupation = occ_ref[o]

        def store(r, new):
            narrow(resp_ref.at[o], r - 4, new)
            term = occupation * orbs_ref[o, r - 4] * resp_ref[o, r - 4]
            dens_ref[r - 4] = term if o == 0 else dens_ref[r - 4] + term

        sweep(b_ref, s_ref, sc_ref, o, 4, store)


def swap_blocks(rows):
    block = lax.broadcasted_iota(jnp.int32, rows[0].shape, rows[0].ndim - 1) // 16
    for d in (1, 2, 4):
        keep = (block // d) % 2 == 0
        out = list(rows)
        for k in range(8):
            if k & d == 0:
                a, b = rows[k], rows[k + d]
                out[k] = jnp.where(keep, a, pltpu.roll(b, 16 * d, 1))
                out[k + d] = jnp.where(keep, pltpu.roll(a, 128 - 16 * d, 1), b)
        rows = out
    return rows


def second_kernel(
    own_ref, other_ref, resp_in_ref, scale_ref, prod_ref, orbs_ref, kerns_ref, occ_ref, place_ref,
    resp_ref, out_ref, p_ref, sc_ref, a_ref, b_ref, dens_ref,
):
    first_core = place_ref[2] == 0
    for r in range(24):
        mine, theirs = own_ref[r % 12], other_ref[r % 12]
        total = jnp.where(first_core, mine, theirs) if r < 12 else jnp.where(first_core, theirs, mine)
        raised = kerns_ref[r] * total
        for o in range(2):
            p_ref[o, r] = prod_ref[o, r] + raised * orbs_ref[o, r]
    for o in range(2):
        sources(p_ref, scale_ref, sc_ref, o)
        sweep(resp_in_ref, scale_ref, sc_ref, o, 1, into(a_ref, o))
        sweep(a_ref, scale_ref, sc_ref, o, 2, into(b_ref, o))
        sweep(b_ref, scale_ref, sc_ref, o, 3, into(a_ref, o))
        occupation = occ_ref[o]

        def store(r, new):
            own = new[:16]
            resp_ref[o, r - 4] = own
            term = occupation * orbs_ref[o, r, 0:16] * own
            dens_ref[r - 4] = term if o == 0 else dens_ref[r - 4] + term

        sweep(a_ref, scale_ref, sc_ref, o, 4, store)
    for part in range(4):
        y, z = part // 2, 8 * (part % 2)
        blocks = swap_blocks([dens_ref[2 * k + y, z : z + 8] for k in range(8)])
        for b in range(8):
            out_ref[b, part] = blocks[b]


def final_kernel(own_ref, one_ref, two_ref, three_ref, dens_ref):
    for part in range(4):
        y, z = part // 2, 8 * (part % 2)
        total = (own_ref[part] + one_ref[part]) + (two_ref[part] + three_ref[part])
        for k in range(8):
            moved = total if k == 0 else pltpu.roll(total, 128 - 16 * k, 1)
            dens_ref[2 * k + y, z : z + 8, :] = moved[:, :16]


def exchange(near, far, axis):
    count = lax.axis_size(axis)
    far = lax.ppermute(far, axis, [(i, (i - 1) % count if i % 2 == 0 else (i + 1) % count) for i in range(count)])
    near = lax.ppermute(near, axis, [(i, i ^ 1) for i in range(count)])
    return near, far


def partner(value, *steps):
    count = lax.axis_size("bands")
    return lax.ppermute(value, "bands", [(i, i ^ steps[i % len(steps)]) for i in range(count)])


def on_device(orbitals, orbital_shift, occupation, potential, perturbation, kernel):
    group = lax.axis_index("bands")
    core, chip = group % 2, group // 2
    place = jnp.stack([lax.axis_index("gy") % 2, lax.axis_index("gz") % 2, core]).astype(jnp.int32)
    arrays = (orbitals, perturbation, potential, kernel)

    strip = f32(Y_ROWS, 16, 128)
    near, far = call(
        strips_kernel, (strip, strip), *arrays, place, smem=1, where=HBM, limit=None,
        scratch=[scratch32(2, 16, 16, 128)] + [scratch32(16, 16, 128)] * 3 + [pltpu.SemaphoreType.DMA((4,))],
    )
    ynear, yfar = exchange(near, far, "gy")
    strip = f32(Z_TILES, 8, 128)
    far, near = call(pack_kernel, (strip, strip), *arrays, ynear, yfar, place, smem=1)
    znear, zfar = exchange(near, far, "gz")
    pair, single = f32(2, 24, 24, 128), f32(24, 24, 128)
    response, partial, scale, products, orbs, kernels = call(
        first_kernel, (pair, single, pair, pair, pair, single),
        *arrays, ynear, yfar, zfar, znear, orbital_shift, occupation, place,
        scratch=[scratch32(2, 32, 32, 128)] * 5 + [scratch32(32, 32, 128)], smem=3,
    )

    own = lax.dynamic_slice_in_dim(partial, 12 * core, 12, 0)
    own = own + partner(lax.dynamic_slice_in_dim(partial, 12 * (1 - core), 12, 0), 1)
    own = own + partner(own, 2, 6)
    own = own + partner(own, 6, 2)
    other = partner(own, 1)
    response, blocks = call(
        second_kernel, (f32(2, 16, 16, 128), f32(8, 4, 8, 128)),
        own, other, response, scale, products, orbs, kernels, occupation, place,
        scratch=[scratch32(2, 24, 24, 128)] * 4 + [scratch32(16, 16, 128)], smem=2,
    )

    blocks = blocks.reshape(4, 2, 4, 8, 128)
    kept = lax.dynamic_index_in_dim(blocks, core, 1, keepdims=False)
    kept = kept + partner(lax.dynamic_index_in_dim(blocks, 1 - core, 1, keepdims=False), 1)

    def block_of(step):
        return lax.dynamic_index_in_dim(kept, chip ^ step, 0, keepdims=False)

    two, one, three = (partner(block_of(step), 2 * step) for step in (2, 1, 3))
    density = call(final_kernel, f32(16, 16, 16), block_of(0), one, two, three)
    return response, density


def solution(mesh):
    placed = (
        P("bands", "gy", "gz", None),
        P("bands"),
        P("bands"),
        P("gy", "gz", None),
        P("gy", "gz", None),
        P("gy", "gz", None),
    )
    return jax.shard_map(
        on_device,
        mesh=mesh,
        in_specs=placed,
        out_specs=(P("bands", "gy", "gz", None), P("gy", "gz", "bands")),
        check_vma=False,
    )
```

```python
import jax
import jax.numpy as jnp
from jax import lax
from jax.experimental import pallas as pl
from jax.experimental.pallas import tpu as pltpu
from jax.sharding import PartitionSpec as P

RELAX = 0.8
HALO = 4
VMEM = pl.BlockSpec(memory_space=pltpu.VMEM)
SMEM = pl.BlockSpec(memory_space=pltpu.SMEM)


def call(body, outs, *args, scratch=(), smem=0):
    return pl.pallas_call(
        body,
        out_shape=outs,
        in_specs=[VMEM] * (len(args) - smem) + [SMEM] * smem,
        out_specs=jax.tree.map(lambda _: VMEM, outs),
        scratch_shapes=list(scratch),
        compiler_params=pltpu.CompilerParams(vmem_limit_bytes=48 * 2**20),
    )(*args)


def f32(*shape):
    return jax.ShapeDtypeStruct(shape, jnp.float32)


def low_half():
    return lax.broadcasted_iota(jnp.int32, (8, 128), 0) < 4


def pack_z(row, even, near_ref, far_ref, field):
    low = low_half()
    for j in range(12):
        a, b = row(j), row(j + 12)
        head = jnp.where(low, a[:8], pltpu.roll(b[:8], 4, 0))
        tail = jnp.where(low, pltpu.roll(b[8:], 4, 0), a[8:])
        near_ref[field, j] = jnp.where(even, tail, head)
        far_ref[field, j] = jnp.where(even, head, tail)


def padded_row(centre_ref, lo_ref, hi_ref, field):
    def row(r):
        if r < 4:
            return lo_ref[field, r]
        if r < 20:
            return centre_ref[field, r - 4]
        return hi_ref[field, r - 20]

    return row


def pack_kernel(centre_ref, lo_ref, hi_ref, odd_ref, far_ref, near_ref):
    even = odd_ref[0] == 0
    for field in range(centre_ref.shape[0]):
        pack_z(padded_row(centre_ref, lo_ref, hi_ref, field), even, near_ref, far_ref, field)


def assemble(row, near_ref, far_ref, field, odd_ref, dest_ref, at):
    low, even = low_half(), odd_ref[0] == 0
    for r in range(24):
        dest_ref[at, r, 0:16] = row(r)
    for j in range(12):
        near, far = near_ref[field, j], far_ref[field, j]
        above, below = jnp.where(even, near, far), jnp.where(even, far, near)
        dest_ref[at, j, 16:24] = jnp.where(low, above, below)
        dest_ref[at, j + 12, 16:24] = pltpu.roll(jnp.where(low, below, above), 4, 0)


def shifts_z(u):
    return pltpu.roll(u, 1, u.ndim - 2) + pltpu.roll(u, 23, u.ndim - 2)


def shifts_x(u):
    return pltpu.roll(u, 1, u.ndim - 1) + pltpu.roll(u, 127, u.ndim - 1)


def by_rows(first, last, load, emit):
    before, at = load(first - 1), load(first)
    for r in range(first, last):
        after = load(r + 1)
        emit(r, before, at, after)
        before, at = at, after


def sources(p_ref, scale_ref, sc_ref, o):
    def load(r):
        return p_ref[o, r]

    def emit(r, before, at, after):
        faces = shifts_x(at) + shifts_z(at) + (before + after)
        sc_ref[o, r] = scale_ref[o, r] * (-30.0 * at - 5.0 * faces)

    by_rows(1, 23, load, emit)


def sweep(src_ref, scale_ref, sc_ref, o, margin, store):
    def load(r):
        u = src_ref[o, r]
        return u, shifts_z(u)

    def emit(r, before, at, after):
        u, along_z = at
        across = before[1] + after[1]
        m = before[0] + after[0] + along_z
        n = 3.0 * m + across
        total = shifts_x(14.0 * u + n) + (3.0 * n + 5.0 * m)
        store(r, 0.2 * u + sc_ref[o, r] + scale_ref[o, r] * total)

    by_rows(margin, 24 - margin, load, emit)


def into(dest_ref, o):
    def store(r, new):
        dest_ref[o, r] = new

    return store


def last_sweep(src_ref, scale_ref, sc_ref, o, orb_ref, occ_ref, resp_ref, dens_ref):
    occupation = occ_ref[o]

    def store(r, new):
        own = new[:16]
        resp_ref[o, r - 4] = own
        term = occupation * orb_ref[o, r - 4] * own
        dens_ref[r - 4] = term if o == 0 else dens_ref[r - 4] + term

    sweep(src_ref, scale_ref, sc_ref, o, 4, store)


def first_kernel(
    centre_ref, lo_ref, hi_ref, far_ref, near_ref, orb_ref, shift_ref, occ_ref, odd_ref,
    resp_ref, dens_ref, scale_ref, p_ref, sc_ref, a_ref, b_ref,
):
    for field in range(2):
        assemble(padded_row(centre_ref, lo_ref, hi_ref, field), near_ref, far_ref, field, odd_ref, p_ref, field)
    assemble(padded_row(centre_ref, lo_ref, hi_ref, 2), near_ref, far_ref, 2, odd_ref, a_ref, 0)
    for o in range(2):
        base = 32.0 / 15.0 + shift_ref[o]

        for r in range(1, 23):
            scale_ref[o, r] = (RELAX / 60.0) / (base + a_ref[0, r])
    for o in range(2):
        sources(p_ref, scale_ref, sc_ref, o)
    for o in range(2):
        sweep(sc_ref, scale_ref, sc_ref, o, 2, into(a_ref, o))
        sweep(a_ref, scale_ref, sc_ref, o, 3, into(b_ref, o))
        last_sweep(b_ref, scale_ref, sc_ref, o, orb_ref, occ_ref, resp_ref, dens_ref)


def change_kernel(own_ref, other_ref, pert_ref, kern_ref, orb_ref, resp_ref, core_ref, centre_ref, up_ref, down_ref):
    first_core = core_ref[0] == 0
    for y in range(16):
        mine, theirs = own_ref[y % 8], other_ref[y % 8]
        total = jnp.where(first_core, mine, theirs) if y < 8 else jnp.where(first_core, theirs, mine)
        change = pert_ref[y] + kern_ref[y] * total
        for o in range(2):
            product, response = change * orb_ref[o, y], resp_ref[o, y]
            centre_ref[o, y] = product
            centre_ref[2 + o, y] = response
            if y < 4:
                down_ref[o, y] = product
                down_ref[2 + o, y] = response
            if y >= 12:
                up_ref[o, y - 12] = product
                up_ref[2 + o, y - 12] = response


def swap_blocks(rows):
    block = lax.broadcasted_iota(jnp.int32, rows[0].shape, rows[0].ndim - 1) // 16
    for d in (1, 2, 4):
        keep = (block // d) % 2 == 0
        out = list(rows)
        for k in range(8):
            if k & d == 0:
                a, b = rows[k], rows[k + d]
                out[k] = jnp.where(keep, a, pltpu.roll(b, 16 * d, 1))
                out[k + d] = jnp.where(keep, pltpu.roll(a, 128 - 16 * d, 1), b)
        rows = out
    return rows


def second_kernel(
    centre_ref, lo_ref, hi_ref, far_ref, near_ref, scale_ref, orb_ref, occ_ref, odd_ref,
    resp_ref, out_ref, p_ref, u_ref, sc_ref, a_ref, b_ref, dens_ref,
):
    for o in range(2):
        assemble(padded_row(centre_ref, lo_ref, hi_ref, o), near_ref, far_ref, o, odd_ref, p_ref, o)
        assemble(padded_row(centre_ref, lo_ref, hi_ref, 2 + o), near_ref, far_ref, 2 + o, odd_ref, u_ref, o)
    for o in range(2):
        sources(p_ref, scale_ref, sc_ref, o)
        sweep(u_ref, scale_ref, sc_ref, o, 1, into(a_ref, o))
        sweep(a_ref, scale_ref, sc_ref, o, 2, into(b_ref, o))
        sweep(b_ref, scale_ref, sc_ref, o, 3, into(a_ref, o))
        last_sweep(a_ref, scale_ref, sc_ref, o, orb_ref, occ_ref, resp_ref, dens_ref)
    for part in range(4):
        y, z = part // 2, 8 * (part % 2)
        blocks = swap_blocks([dens_ref[2 * k + y, z : z + 8] for k in range(8)])
        for b in range(8):
            out_ref[b, part] = blocks[b]


def final_kernel(own_ref, one_ref, two_ref, three_ref, dens_ref):
    for part in range(4):
        y, z = part // 2, 8 * (part % 2)
        total = (own_ref[part] + one_ref[part]) + (two_ref[part] + three_ref[part])
        for k in range(8):
            moved = total if k == 0 else pltpu.roll(total, 128 - 16 * k, 1)
            dens_ref[2 * k + y, z : z + 8, :] = moved[:, :16]


def ring(axis, step):
    count = lax.axis_size(axis)
    return [(i, (i + step) % count) for i in range(count)]


def exchange_y(up, down):
    return lax.ppermute(up, "gy", ring("gy", 1)), lax.ppermute(down, "gy", ring("gy", -1))


def exchange_z(centre, lo, hi, odd):
    fields = centre.shape[0]
    strip = f32(fields, 12, 8, 128)
    far, near = call(pack_kernel, (strip, strip), centre, lo, hi, odd, smem=1)
    count = lax.axis_size("gz")
    far = lax.ppermute(far, "gz", far_pairs(count))
    near = lax.ppermute(near, "gz", [(i, i ^ 1) for i in range(count)])
    return near, far


def far_pairs(count):
    return [(i, (i - 1) % count if i % 2 == 0 else (i + 1) % count) for i in range(count)]


def partner(value, *steps):
    count = lax.axis_size("bands")
    return lax.ppermute(value, "bands", [(i, i ^ steps[i % len(steps)]) for i in range(count)])


def on_device(orbitals, orbital_shift, occupation, potential, perturbation, kernel):
    group = lax.axis_index("bands")
    core, chip = group % 2, group // 2
    padded = f32(2, 24, 24, 128)
    wide = pltpu.VMEM((2, 24, 24, 128), jnp.float32)

    odd = (lax.axis_index("gz") % 2)[None].astype(jnp.int32)
    def ends(field):
        return field[12:16], field[0:4]

    edges = lax.optimization_barrier([ends(field) for field in (perturbation, potential, orbitals[0], orbitals[1])])
    up, down = (
        jnp.stack([edges[0][i] * edges[2][i], edges[0][i] * edges[3][i], edges[1][i]]) for i in range(2)
    )
    centre = jnp.concatenate([perturbation[None] * orbitals, potential[None]], 0)
    lo, hi = exchange_y(up, down)
    near, far = exchange_z(centre, lo, hi, odd)
    response, partial, scale = call(
        first_kernel, (f32(2, 16, 16, 128), f32(16, 16, 128), padded),
        centre, lo, hi, far, near, orbitals, orbital_shift, occupation, odd,
        scratch=[wide] * 4, smem=3,
    )

    own = lax.dynamic_slice_in_dim(partial, 8 * core, 8, 0)
    own = own + partner(lax.dynamic_slice_in_dim(partial, 8 * (1 - core), 8, 0), 1)
    own = own + partner(own, 2, 6)
    own = own + partner(own, 6, 2)
    other = partner(own, 1)
    centre, up, down = call(
        change_kernel, (f32(4, 16, 16, 128), f32(4, 4, 16, 128), f32(4, 4, 16, 128)),
        own, other, perturbation, kernel, orbitals, response, core[None].astype(jnp.int32), smem=1,
    )
    lo, hi = exchange_y(up, down)
    near, far = exchange_z(centre, lo, hi, odd)
    response, blocks = call(
        second_kernel, (f32(2, 16, 16, 128), f32(8, 4, 8, 128)),
        centre, lo, hi, far, near, scale, orbitals, occupation, odd,
        scratch=[wide] * 5 + [pltpu.VMEM((16, 16, 128), jnp.float32)], smem=2,
    )

    blocks = blocks.reshape(4, 2, 4, 8, 128)
    kept = lax.dynamic_index_in_dim(blocks, core, 1, keepdims=False)
    kept = kept + partner(lax.dynamic_index_in_dim(blocks, 1 - core, 1, keepdims=False), 1)

    def block_of(step):
        return lax.dynamic_index_in_dim(kept, chip ^ step, 0, keepdims=False)

    two, one, three = (partner(block_of(step), 2 * step) for step in (2, 1, 3))
    density = call(final_kernel, f32(16, 16, 16), block_of(0), one, two, three)
    return response, density


def solution(mesh):
    placed = (
        P("bands", "gy", "gz", None),
        P("bands"),
        P("bands"),
        P("gy", "gz", None),
        P("gy", "gz", None),
        P("gy", "gz", None),
    )
    return jax.shard_map(
        on_device,
        mesh=mesh,
        in_specs=placed,
        out_specs=(P("bands", "gy", "gz", None), P("gy", "gz", "bands")),
        check_vma=False,
    )
```

```python
import jax
import jax.numpy as jnp
from jax import lax
from jax.experimental import pallas as pl
from jax.experimental.pallas import tpu as pltpu
from jax.sharding import PartitionSpec as P

RELAX = 0.8
HALO = 4
VMEM = pl.BlockSpec(memory_space=pltpu.VMEM)
SMEM = pl.BlockSpec(memory_space=pltpu.SMEM)


def call(body, outs, *args, scratch=(), smem=0):
    return pl.pallas_call(
        body,
        out_shape=outs,
        in_specs=[VMEM] * (len(args) - smem) + [SMEM] * smem,
        out_specs=jax.tree.map(lambda _: VMEM, outs),
        scratch_shapes=list(scratch),
        compiler_params=pltpu.CompilerParams(vmem_limit_bytes=48 * 2**20),
    )(*args)


def f32(*shape):
    return jax.ShapeDtypeStruct(shape, jnp.float32)


def low_half():
    return lax.broadcasted_iota(jnp.int32, (8, 128), 0) < 4


def pack_z(row, even, near_ref, far_ref, field):
    low = low_half()
    for j in range(12):
        a, b = row(j), row(j + 12)
        head = jnp.where(low, a[:8], pltpu.roll(b[:8], 4, 0))
        tail = jnp.where(low, pltpu.roll(b[8:], 4, 0), a[8:])
        near_ref[field, j] = jnp.where(even, tail, head)
        far_ref[field, j] = jnp.where(even, head, tail)


def padded_row(centre_ref, lo_ref, hi_ref, field):
    def row(r):
        if r < 4:
            return lo_ref[field, r]
        if r < 20:
            return centre_ref[field, r - 4]
        return hi_ref[field, r - 20]

    return row


def pack_kernel(centre_ref, lo_ref, hi_ref, odd_ref, far_ref, near_ref):
    even = odd_ref[0] == 0
    for field in range(centre_ref.shape[0]):
        pack_z(padded_row(centre_ref, lo_ref, hi_ref, field), even, near_ref, far_ref, field)


def assemble(row, near_ref, far_ref, field, odd_ref, dest_ref, at):
    low, even = low_half(), odd_ref[0] == 0
    for r in range(24):
        dest_ref[at, r, 0:16] = row(r)
    for j in range(12):
        near, far = near_ref[field, j], far_ref[field, j]
        above, below = jnp.where(even, near, far), jnp.where(even, far, near)
        dest_ref[at, j, 16:24] = jnp.where(low, above, below)
        dest_ref[at, j + 12, 16:24] = pltpu.roll(jnp.where(low, below, above), 4, 0)


def shifts_z(u):
    return pltpu.roll(u, 1, u.ndim - 2) + pltpu.roll(u, 23, u.ndim - 2)


def shifts_x(u):
    return pltpu.roll(u, 1, u.ndim - 1) + pltpu.roll(u, 127, u.ndim - 1)


def by_rows(first, last, load, emit):
    before, at = load(first - 1), load(first)
    for r in range(first, last):
        after = load(r + 1)
        emit(r, before, at, after)
        before, at = at, after


def sources(p_ref, scale_ref, sc_ref, o):
    def load(r):
        return p_ref[o, r]

    def emit(r, before, at, after):
        faces = shifts_x(at) + shifts_z(at) + (before + after)
        sc_ref[o, r] = scale_ref[o, r] * (-30.0 * at - 5.0 * faces)

    by_rows(1, 23, load, emit)


def sweep(src_ref, scale_ref, sc_ref, o, margin, store):
    def load(r):
        u = src_ref[o, r]
        return u, shifts_z(u)

    def emit(r, before, at, after):
        u, along_z = at
        across = before[1] + after[1]
        m = before[0] + after[0] + along_z
        n = 3.0 * m + across
        total = shifts_x(14.0 * u + n) + (3.0 * n + 5.0 * m)
        store(r, 0.2 * u + sc_ref[o, r] + scale_ref[o, r] * total)

    by_rows(margin, 24 - margin, load, emit)


def into(dest_ref, o):
    def store(r, new):
        dest_ref[o, r] = new

    return store


def last_sweep(src_ref, scale_ref, sc_ref, o, orb_ref, occ_ref, resp_ref, dens_ref):
    occupation = occ_ref[o]

    def store(r, new):
        own = new[:16]
        resp_ref[o, r - 4] = own
        term = occupation * orb_ref[o, r - 4] * own
        dens_ref[r - 4] = term if o == 0 else dens_ref[r - 4] + term

    sweep(src_ref, scale_ref, sc_ref, o, 4, store)


def first_kernel(
    centre_ref, lo_ref, hi_ref, far_ref, near_ref, orb_ref, shift_ref, occ_ref, odd_ref,
    resp_ref, dens_ref, scale_ref, p_ref, sc_ref, a_ref, b_ref,
):
    for field in range(2):
        assemble(padded_row(centre_ref, lo_ref, hi_ref, field), near_ref, far_ref, field, odd_ref, p_ref, field)
    assemble(padded_row(centre_ref, lo_ref, hi_ref, 2), near_ref, far_ref, 2, odd_ref, a_ref, 0)
    for o in range(2):
        base = 32.0 / 15.0 + shift_ref[o]

        for r in range(1, 23):
            scale_ref[o, r] = (RELAX / 60.0) / (base + a_ref[0, r])
    for o in range(2):
        sources(p_ref, scale_ref, sc_ref, o)
    for o in range(2):
        sweep(sc_ref, scale_ref, sc_ref, o, 2, into(a_ref, o))
        sweep(a_ref, scale_ref, sc_ref, o, 3, into(b_ref, o))
        last_sweep(b_ref, scale_ref, sc_ref, o, orb_ref, occ_ref, resp_ref, dens_ref)


def strips_kernel(*refs):
    perturbation, potential, orbitals, dests = refs[0:2], refs[2:4], (refs[4:6], refs[6:8]), refs[8:10]
    for end, dest_ref in enumerate(dests):
        for y in range(4):
            for o in range(2):
                dest_ref[o, y] = perturbation[end][y] * orbitals[o][end][y]
            dest_ref[2, y] = potential[end][y]


def change_kernel(own_ref, other_ref, pert_ref, kern_ref, orb_ref, resp_ref, core_ref, centre_ref, up_ref, down_ref):
    first_core = core_ref[0] == 0
    for y in range(16):
        mine, theirs = own_ref[y % 8], other_ref[y % 8]
        total = jnp.where(first_core, mine, theirs) if y < 8 else jnp.where(first_core, theirs, mine)
        change = pert_ref[y] + kern_ref[y] * total
        for o in range(2):
            product, response = change * orb_ref[o, y], resp_ref[o, y]
            centre_ref[o, y] = product
            centre_ref[2 + o, y] = response
            if y < 4:
                down_ref[o, y] = product
                down_ref[2 + o, y] = response
            if y >= 12:
                up_ref[o, y - 12] = product
                up_ref[2 + o, y - 12] = response


def swap_blocks(rows):
    block = lax.broadcasted_iota(jnp.int32, rows[0].shape, rows[0].ndim - 1) // 16
    for d in (1, 2, 4):
        keep = (block // d) % 2 == 0
        out = list(rows)
        for k in range(8):
            if k & d == 0:
                a, b = rows[k], rows[k + d]
                out[k] = jnp.where(keep, a, pltpu.roll(b, 16 * d, 1))
                out[k + d] = jnp.where(keep, pltpu.roll(a, 128 - 16 * d, 1), b)
        rows = out
    return rows


def second_kernel(
    centre_ref, lo_ref, hi_ref, far_ref, near_ref, scale_ref, orb_ref, occ_ref, odd_ref,
    resp_ref, out_ref, p_ref, u_ref, sc_ref, a_ref, b_ref, dens_ref,
):
    for o in range(2):
        assemble(padded_row(centre_ref, lo_ref, hi_ref, o), near_ref, far_ref, o, odd_ref, p_ref, o)
        assemble(padded_row(centre_ref, lo_ref, hi_ref, 2 + o), near_ref, far_ref, 2 + o, odd_ref, u_ref, o)
    for o in range(2):
        sources(p_ref, scale_ref, sc_ref, o)
        sweep(u_ref, scale_ref, sc_ref, o, 1, into(a_ref, o))
        sweep(a_ref, scale_ref, sc_ref, o, 2, into(b_ref, o))
        sweep(b_ref, scale_ref, sc_ref, o, 3, into(a_ref, o))
        last_sweep(a_ref, scale_ref, sc_ref, o, orb_ref, occ_ref, resp_ref, dens_ref)
    for part in range(4):
        y, z = part // 2, 8 * (part % 2)
        blocks = swap_blocks([dens_ref[2 * k + y, z : z + 8] for k in range(8)])
        for b in range(8):
            out_ref[b, part] = blocks[b]


def final_kernel(own_ref, one_ref, two_ref, three_ref, resp_ref, dens_ref, response_ref):
    response_ref[...] = resp_ref[...]
    for part in range(4):
        y, z = part // 2, 8 * (part % 2)
        total = (own_ref[part] + one_ref[part]) + (two_ref[part] + three_ref[part])
        for k in range(8):
            moved = total if k == 0 else pltpu.roll(total, 128 - 16 * k, 1)
            dens_ref[2 * k + y, z : z + 8, :] = moved[:, :16]


def ring(axis, step):
    count = lax.axis_size(axis)
    return [(i, (i + step) % count) for i in range(count)]


def exchange_y(up, down):
    return lax.ppermute(up, "gy", ring("gy", 1)), lax.ppermute(down, "gy", ring("gy", -1))


def exchange_z(centre, lo, hi, odd):
    fields = centre.shape[0]
    strip = f32(fields, 12, 8, 128)
    far, near = call(pack_kernel, (strip, strip), centre, lo, hi, odd, smem=1)
    count = lax.axis_size("gz")
    far = lax.ppermute(far, "gz", far_pairs(count))
    near = lax.ppermute(near, "gz", [(i, i ^ 1) for i in range(count)])
    return near, far


def far_pairs(count):
    return [(i, (i - 1) % count if i % 2 == 0 else (i + 1) % count) for i in range(count)]


def partner(value, *steps):
    count = lax.axis_size("bands")
    return lax.ppermute(value, "bands", [(i, i ^ steps[i % len(steps)]) for i in range(count)])


def on_device(orbitals, orbital_shift, occupation, potential, perturbation, kernel):
    group = lax.axis_index("bands")
    core, chip = group % 2, group // 2
    padded = f32(2, 24, 24, 128)
    wide = pltpu.VMEM((2, 24, 24, 128), jnp.float32)

    odd = (lax.axis_index("gz") % 2)[None].astype(jnp.int32)
    def ends(field):
        return field[12:16], field[0:4]

    edges = lax.optimization_barrier([ends(field) for field in (perturbation, potential, orbitals[0], orbitals[1])])
    up, down = call(strips_kernel, (f32(3, 4, 16, 128), f32(3, 4, 16, 128)), *(end for pair in edges for end in pair))
    centre = jnp.concatenate([perturbation[None] * orbitals, potential[None]], 0)
    lo, hi = exchange_y(up, down)
    near, far = exchange_z(centre, lo, hi, odd)
    response, partial, scale = call(
        first_kernel, (f32(2, 16, 16, 128), f32(16, 16, 128), padded),
        centre, lo, hi, far, near, orbitals, orbital_shift, occupation, odd,
        scratch=[wide] * 4, smem=3,
    )

    own = lax.dynamic_slice_in_dim(partial, 8 * core, 8, 0)
    own = own + partner(lax.dynamic_slice_in_dim(partial, 8 * (1 - core), 8, 0), 1)
    own = own + partner(own, 2, 6)
    own = own + partner(own, 6, 2)
    other = partner(own, 1)
    centre, up, down = call(
        change_kernel, (f32(4, 16, 16, 128), f32(4, 4, 16, 128), f32(4, 4, 16, 128)),
        own, other, perturbation, kernel, orbitals, response, core[None].astype(jnp.int32), smem=1,
    )
    lo, hi = exchange_y(up, down)
    near, far = exchange_z(centre, lo, hi, odd)
    response, blocks = call(
        second_kernel, (f32(2, 16, 16, 128), f32(8, 4, 8, 128)),
        centre, lo, hi, far, near, scale, orbitals, occupation, odd,
        scratch=[wide] * 5 + [pltpu.VMEM((16, 16, 128), jnp.float32)], smem=2,
    )

    blocks = blocks.reshape(4, 2, 4, 8, 128)
    kept = lax.dynamic_index_in_dim(blocks, core, 1, keepdims=False)
    kept = kept + partner(lax.dynamic_index_in_dim(blocks, 1 - core, 1, keepdims=False), 1)

    def block_of(step):
        return lax.dynamic_index_in_dim(kept, chip ^ step, 0, keepdims=False)

    two, one, three = (partner(block_of(step), 2 * step) for step in (2, 1, 3))
    density, response = call(
        final_kernel, (f32(16, 16, 16), f32(2, 16, 16, 128)), block_of(0), one, two, three, response
    )
    return response, density


def solution(mesh):
    placed = (
        P("bands", "gy", "gz", None),
        P("bands"),
        P("bands"),
        P("gy", "gz", None),
        P("gy", "gz", None),
        P("gy", "gz", None),
    )
    return jax.shard_map(
        on_device,
        mesh=mesh,
        in_specs=placed,
        out_specs=(P("bands", "gy", "gz", None), P("gy", "gz", "bands")),
        check_vma=False,
    )
```

```python
import jax
import jax.numpy as jnp
from jax import lax
from jax.experimental import pallas as pl
from jax.experimental.pallas import tpu as pltpu
from jax.sharding import PartitionSpec as P

RELAX = 0.8
HALO = 4
VMEM = pl.BlockSpec(memory_space=pltpu.VMEM)
SMEM = pl.BlockSpec(memory_space=pltpu.SMEM)


def call(body, outs, *args, scratch=(), smem=0):
    return pl.pallas_call(
        body,
        out_shape=outs,
        in_specs=[VMEM] * (len(args) - smem) + [SMEM] * smem,
        out_specs=jax.tree.map(lambda _: VMEM, outs),
        scratch_shapes=list(scratch),
        compiler_params=pltpu.CompilerParams(vmem_limit_bytes=48 * 2**20),
    )(*args)


def f32(*shape):
    return jax.ShapeDtypeStruct(shape, jnp.float32)


def low_half():
    return lax.broadcasted_iota(jnp.int32, (8, 128), 0) < 4


def pack_z(row, head_ref, tail_ref, field):
    low = low_half()
    for j in range(12):
        a, b = row(j), row(j + 12)
        head_ref[field, j] = jnp.where(low, a[:8], pltpu.roll(b[:8], 4, 0))
        tail_ref[field, j] = jnp.where(low, pltpu.roll(b[8:], 4, 0), a[8:])


def padded_row(centre_ref, lo_ref, hi_ref, field):
    def row(r):
        if r < 4:
            return lo_ref[field, r]
        if r < 20:
            return centre_ref[field, r - 4]
        return hi_ref[field, r - 20]

    return row


def pack_kernel(centre_ref, lo_ref, hi_ref, tail_ref, head_ref):
    for field in range(centre_ref.shape[0]):
        pack_z(padded_row(centre_ref, lo_ref, hi_ref, field), head_ref, tail_ref, field)


def assemble(row, above_ref, below_ref, field, dest_ref, at):
    low = low_half()
    for r in range(24):
        dest_ref[at, r, 0:16] = row(r)
    for j in range(12):
        above, below = above_ref[field, j], below_ref[field, j]
        dest_ref[at, j, 16:24] = jnp.where(low, above, below)
        dest_ref[at, j + 12, 16:24] = pltpu.roll(jnp.where(low, below, above), 4, 0)


def shifts_z(u):
    return pltpu.roll(u, 1, u.ndim - 2) + pltpu.roll(u, 23, u.ndim - 2)


def shifts_x(u):
    return pltpu.roll(u, 1, u.ndim - 1) + pltpu.roll(u, 127, u.ndim - 1)


def by_rows(first, last, load, emit):
    before, at = load(first - 1), load(first)
    for r in range(first, last):
        after = load(r + 1)
        emit(r, before, at, after)
        before, at = at, after


def sources(p_ref, scale_ref, sc_ref, o):
    def load(r):
        return p_ref[o, r]

    def emit(r, before, at, after):
        faces = shifts_x(at) + shifts_z(at) + (before + after)
        sc_ref[o, r] = scale_ref[o, r] * (-30.0 * at - 5.0 * faces)

    by_rows(1, 23, load, emit)


def sweep(src_ref, scale_ref, sc_ref, o, margin, store):
    def load(r):
        u = src_ref[o, r]
        return u, shifts_z(u)

    def emit(r, before, at, after):
        u, along_z = at
        across = before[1] + after[1]
        m = before[0] + after[0] + along_z
        n = 3.0 * m + across
        total = shifts_x(14.0 * u + n) + (3.0 * n + 5.0 * m)
        store(r, 0.2 * u + sc_ref[o, r] + scale_ref[o, r] * total)

    by_rows(margin, 24 - margin, load, emit)


def into(dest_ref, o):
    def store(r, new):
        dest_ref[o, r] = new

    return store


def last_sweep(src_ref, scale_ref, sc_ref, o, orb_ref, occ_ref, resp_ref, dens_ref):
    occupation = occ_ref[o]

    def store(r, new):
        own = new[:16]
        resp_ref[o, r - 4] = own
        term = occupation * orb_ref[o, r - 4] * own
        dens_ref[r - 4] = term if o == 0 else dens_ref[r - 4] + term

    sweep(src_ref, scale_ref, sc_ref, o, 4, store)


def first_kernel(
    centre_ref, lo_ref, hi_ref, below_ref, above_ref, orb_ref, shift_ref, occ_ref,
    resp_ref, dens_ref, scale_ref, p_ref, sc_ref, a_ref, b_ref,
):
    for field in range(2):
        assemble(padded_row(centre_ref, lo_ref, hi_ref, field), above_ref, below_ref, field, p_ref, field)
    assemble(padded_row(centre_ref, lo_ref, hi_ref, 2), above_ref, below_ref, 2, a_ref, 0)
    for o in range(2):
        base = 32.0 / 15.0 + shift_ref[o]

        for r in range(1, 23):
            scale_ref[o, r] = (RELAX / 60.0) / (base + a_ref[0, r])
    for o in range(2):
        sources(p_ref, scale_ref, sc_ref, o)
    for o in range(2):
        sweep(sc_ref, scale_ref, sc_ref, o, 2, into(a_ref, o))
        sweep(a_ref, scale_ref, sc_ref, o, 3, into(b_ref, o))
        last_sweep(b_ref, scale_ref, sc_ref, o, orb_ref, occ_ref, resp_ref, dens_ref)


def strips_kernel(*refs):
    perturbation, potential, orbitals, dests = refs[0:2], refs[2:4], (refs[4:6], refs[6:8]), refs[8:10]
    for end, dest_ref in enumerate(dests):
        for y in range(4):
            for o in range(2):
                dest_ref[o, y] = perturbation[end][y] * orbitals[o][end][y]
            dest_ref[2, y] = potential[end][y]


def change_kernel(own_ref, other_ref, pert_ref, kern_ref, orb_ref, resp_ref, core_ref, centre_ref, up_ref, down_ref):
    first_core = core_ref[0] == 0
    for y in range(16):
        mine, theirs = own_ref[y % 8], other_ref[y % 8]
        total = jnp.where(first_core, mine, theirs) if y < 8 else jnp.where(first_core, theirs, mine)
        change = pert_ref[y] + kern_ref[y] * total
        for o in range(2):
            product, response = change * orb_ref[o, y], resp_ref[o, y]
            centre_ref[o, y] = product
            centre_ref[2 + o, y] = response
            if y < 4:
                down_ref[o, y] = product
                down_ref[2 + o, y] = response
            if y >= 12:
                up_ref[o, y - 12] = product
                up_ref[2 + o, y - 12] = response


def swap_blocks(rows):
    block = lax.broadcasted_iota(jnp.int32, rows[0].shape, rows[0].ndim - 1) // 16
    for d in (1, 2, 4):
        keep = (block // d) % 2 == 0
        out = list(rows)
        for k in range(8):
            if k & d == 0:
                a, b = rows[k], rows[k + d]
                out[k] = jnp.where(keep, a, pltpu.roll(b, 16 * d, 1))
                out[k + d] = jnp.where(keep, pltpu.roll(a, 128 - 16 * d, 1), b)
        rows = out
    return rows


def second_kernel(
    centre_ref, lo_ref, hi_ref, below_ref, above_ref, scale_ref, orb_ref, occ_ref,
    resp_ref, out_ref, p_ref, u_ref, sc_ref, a_ref, b_ref, dens_ref,
):
    for o in range(2):
        assemble(padded_row(centre_ref, lo_ref, hi_ref, o), above_ref, below_ref, o, p_ref, o)
        assemble(padded_row(centre_ref, lo_ref, hi_ref, 2 + o), above_ref, below_ref, 2 + o, u_ref, o)
    for o in range(2):
        sources(p_ref, scale_ref, sc_ref, o)
        sweep(u_ref, scale_ref, sc_ref, o, 1, into(a_ref, o))
        sweep(a_ref, scale_ref, sc_ref, o, 2, into(b_ref, o))
        sweep(b_ref, scale_ref, sc_ref, o, 3, into(a_ref, o))
        last_sweep(a_ref, scale_ref, sc_ref, o, orb_ref, occ_ref, resp_ref, dens_ref)
    for part in range(4):
        y, z = part // 2, 8 * (part % 2)
        blocks = swap_blocks([dens_ref[2 * k + y, z : z + 8] for k in range(8)])
        for b in range(8):
            out_ref[b, part] = blocks[b]


def final_kernel(own_ref, last_ref, resp_ref, dens_ref, response_ref):
    response_ref[...] = resp_ref[...]
    for part in range(4):
        y, z = part // 2, 8 * (part % 2)
        total = own_ref[part] + last_ref[part]
        for k in range(8):
            moved = total if k == 0 else pltpu.roll(total, 128 - 16 * k, 1)
            dens_ref[2 * k + y, z : z + 8, :] = moved[:, :16]


def ring(axis, step):
    count = lax.axis_size(axis)
    return [(i, (i + step) % count) for i in range(count)]


def exchange_y(up, down):
    return lax.ppermute(up, "gy", ring("gy", 1)), lax.ppermute(down, "gy", ring("gy", -1))


def exchange_z(centre, lo, hi):
    fields = centre.shape[0]
    strip = f32(fields, 12, 8, 128)
    tail, head = call(pack_kernel, (strip, strip), centre, lo, hi)
    return lax.ppermute(head, "gz", ring("gz", -1)), lax.ppermute(tail, "gz", ring("gz", 1))


def partner(value, *steps):
    count = lax.axis_size("bands")
    return lax.ppermute(value, "bands", [(i, i ^ steps[i % len(steps)]) for i in range(count)])


def on_device(orbitals, orbital_shift, occupation, potential, perturbation, kernel):
    group = lax.axis_index("bands")
    core, chip = group % 2, group // 2
    padded = f32(2, 24, 24, 128)
    wide = pltpu.VMEM((2, 24, 24, 128), jnp.float32)

    def ends(field):
        return field[12:16], field[0:4]

    edges = lax.optimization_barrier([ends(field) for field in (perturbation, potential, orbitals[0], orbitals[1])])
    up, down = call(strips_kernel, (f32(3, 4, 16, 128), f32(3, 4, 16, 128)), *(end for pair in edges for end in pair))
    centre = jnp.concatenate([perturbation[None] * orbitals, potential[None]], 0)
    lo, hi = exchange_y(up, down)
    above, below = exchange_z(centre, lo, hi)
    response, partial, scale = call(
        first_kernel, (f32(2, 16, 16, 128), f32(16, 16, 128), padded),
        centre, lo, hi, below, above, orbitals, orbital_shift, occupation,
        scratch=[wide] * 4, smem=2,
    )

    own = lax.dynamic_slice_in_dim(partial, 8 * core, 8, 0)
    own = own + partner(lax.dynamic_slice_in_dim(partial, 8 * (1 - core), 8, 0), 1)
    own = own + partner(own, 2, 6)
    own = own + partner(own, 6, 2)
    other = partner(own, 1)
    centre, up, down = call(
        change_kernel, (f32(4, 16, 16, 128), f32(4, 4, 16, 128), f32(4, 4, 16, 128)),
        own, other, perturbation, kernel, orbitals, response, core[None].astype(jnp.int32), smem=1,
    )
    lo, hi = exchange_y(up, down)
    above, below = exchange_z(centre, lo, hi)
    response, blocks = call(
        second_kernel, (f32(2, 16, 16, 128), f32(8, 4, 8, 128)),
        centre, lo, hi, below, above, scale, orbitals, occupation,
        scratch=[wide] * 5 + [pltpu.VMEM((16, 16, 128), jnp.float32)], smem=1,
    )

    blocks = blocks.reshape(4, 2, 4, 8, 128)
    kept = lax.dynamic_index_in_dim(blocks, core, 1, keepdims=False)
    kept = kept + partner(lax.dynamic_index_in_dim(blocks, 1 - core, 1, keepdims=False), 1)

    def block_of(step):
        return lax.dynamic_index_in_dim(kept, chip ^ step, 0, keepdims=False)

    first, second = 1 + 2 * core, 3 - 2 * core
    pair = jnp.stack([block_of(0), block_of(second)]) + partner(jnp.stack([block_of(first), block_of(2)]), 2, 6)
    last = partner(pair[1], 6, 2)
    density, response = call(
        final_kernel, (f32(16, 16, 16), f32(2, 16, 16, 128)), pair[0], last, response
    )
    return response, density


def solution(mesh):
    placed = (
        P("bands", "gy", "gz", None),
        P("bands"),
        P("bands"),
        P("gy", "gz", None),
        P("gy", "gz", None),
        P("gy", "gz", None),
    )
    return jax.shard_map(
        on_device,
        mesh=mesh,
        in_specs=placed,
        out_specs=(P("bands", "gy", "gz", None), P("gy", "gz", "bands")),
        check_vma=False,
    )
```

```python
import jax
import jax.numpy as jnp
from jax import lax
from jax.experimental import pallas as pl
from jax.experimental.pallas import tpu as pltpu
from jax.sharding import PartitionSpec as P

RELAX = 0.8
HALO = 4
VMEM = pl.BlockSpec(memory_space=pltpu.VMEM)
SMEM = pl.BlockSpec(memory_space=pltpu.SMEM)


def call(body, outs, *args, scratch=(), smem=0):
    return pl.pallas_call(
        body,
        out_shape=outs,
        in_specs=[VMEM] * (len(args) - smem) + [SMEM] * smem,
        out_specs=jax.tree.map(lambda _: VMEM, outs),
        scratch_shapes=list(scratch),
        compiler_params=pltpu.CompilerParams(vmem_limit_bytes=48 * 2**20),
    )(*args)


def f32(*shape):
    return jax.ShapeDtypeStruct(shape, jnp.float32)


def low_half():
    return lax.broadcasted_iota(jnp.int32, (8, 128), 0) < 4


def pack_z(row, head_ref, tail_ref, field):
    low = low_half()
    for j in range(12):
        a, b = row(j), row(j + 12)
        head_ref[field, j] = jnp.where(low, a[:8], pltpu.roll(b[:8], 4, 0))
        tail_ref[field, j] = jnp.where(low, pltpu.roll(b[8:], 4, 0), a[8:])


def padded_row(centre_ref, lo_ref, hi_ref, field):
    def row(r):
        if r < 4:
            return lo_ref[field, r]
        if r < 20:
            return centre_ref[field, r - 4]
        return hi_ref[field, r - 20]

    return row


def pack_kernel(centre_ref, lo_ref, hi_ref, tail_ref, head_ref):
    for field in range(centre_ref.shape[0]):
        pack_z(padded_row(centre_ref, lo_ref, hi_ref, field), head_ref, tail_ref, field)


def assemble(row, above_ref, below_ref, field, dest_ref, at):
    for r in range(24):
        dest_ref[at, r, 8:24] = row(r)
    for j in range(12):
        above, below = above_ref[field, j], below_ref[field, j]
        dest_ref[at, j, 24:32] = above
        dest_ref[at, j, 0:8] = below
        dest_ref[at, j + 12, 24:32] = pltpu.roll(above, 4, 0)
        dest_ref[at, j + 12, 0:8] = pltpu.roll(below, 4, 0)


def window(zero, last=False):
    first, count = (8, 16) if last else (4, 24)
    return [pl.ds(zero + first + k, count) for k in (0, -1, 1)]


def shifts_x(u):
    return pltpu.roll(u, 1, u.ndim - 1) + pltpu.roll(u, 127, u.ndim - 1)


def by_rows(first, last, load, emit):
    before, at = load(first - 1), load(first)
    for r in range(first, last):
        after = load(r + 1)
        emit(r, before, at, after)
        before, at = at, after


def sources(p_ref, scale_ref, sc_ref, o, zero):
    here, down, up = window(zero)

    def load(r):
        return p_ref[o, r, here]

    def emit(r, before, at, after):
        faces = shifts_x(at) + (p_ref[o, r, down] + p_ref[o, r, up]) + (before + after)
        sc_ref[o, r, here] = scale_ref[o, r, here] * (-30.0 * at - 5.0 * faces)

    by_rows(1, 23, load, emit)


def sweep(src_ref, scale_ref, sc_ref, o, zero, margin, store):
    here, down, up = window(zero, margin == 4)

    def load(r):
        return src_ref[o, r, here], src_ref[o, r, down] + src_ref[o, r, up]

    def emit(r, before, at, after):
        u, along_z = at
        across = before[1] + after[1]
        m = before[0] + after[0] + along_z
        n = 3.0 * m + across
        total = shifts_x(14.0 * u + n) + (3.0 * n + 5.0 * m)
        store(r, 0.2 * u + sc_ref[o, r, here] + scale_ref[o, r, here] * total)

    by_rows(margin, 24 - margin, load, emit)


def into(dest_ref, o, zero):
    here = window(zero)[0]

    def store(r, new):
        dest_ref[o, r, here] = new

    return store


def last_sweep(src_ref, scale_ref, sc_ref, o, zero, orb_ref, occ_ref, resp_ref, dens_ref):
    occupation = occ_ref[o]

    def store(r, new):
        resp_ref[o, r - 4] = new
        term = occupation * orb_ref[o, r - 4] * new
        dens_ref[r - 4] = term if o == 0 else dens_ref[r - 4] + term

    sweep(src_ref, scale_ref, sc_ref, o, zero, 4, store)


def first_kernel(
    centre_ref, lo_ref, hi_ref, below_ref, above_ref, orb_ref, shift_ref, occ_ref, zero_ref,
    resp_ref, dens_ref, scale_ref, p_ref, sc_ref, a_ref, b_ref,
):
    zero = zero_ref[0]
    for field in range(2):
        assemble(padded_row(centre_ref, lo_ref, hi_ref, field), above_ref, below_ref, field, p_ref, field)
    assemble(padded_row(centre_ref, lo_ref, hi_ref, 2), above_ref, below_ref, 2, a_ref, 0)
    for o in range(2):
        base = 32.0 / 15.0 + shift_ref[o]

        for r in range(1, 23):
            scale_ref[o, r, 0:32] = (RELAX / 60.0) / (base + a_ref[0, r, 0:32])
    for o in range(2):
        sources(p_ref, scale_ref, sc_ref, o, zero)
    for o in range(2):
        sweep(sc_ref, scale_ref, sc_ref, o, zero, 2, into(a_ref, o, zero))
        sweep(a_ref, scale_ref, sc_ref, o, zero, 3, into(b_ref, o, zero))
        last_sweep(b_ref, scale_ref, sc_ref, o, zero, orb_ref, occ_ref, resp_ref, dens_ref)


def strips_kernel(*refs):
    perturbation, potential, orbitals, dests = refs[0:2], refs[2:4], (refs[4:6], refs[6:8]), refs[8:10]
    for end, dest_ref in enumerate(dests):
        for y in range(4):
            for o in range(2):
                dest_ref[o, y] = perturbation[end][y] * orbitals[o][end][y]
            dest_ref[2, y] = potential[end][y]


def change_kernel(own_ref, other_ref, pert_ref, kern_ref, orb_ref, resp_ref, core_ref, centre_ref, up_ref, down_ref):
    first_core = core_ref[0] == 0
    for y in range(16):
        mine, theirs = own_ref[y % 8], other_ref[y % 8]
        total = jnp.where(first_core, mine, theirs) if y < 8 else jnp.where(first_core, theirs, mine)
        change = pert_ref[y] + kern_ref[y] * total
        for o in range(2):
            product, response = change * orb_ref[o, y], resp_ref[o, y]
            centre_ref[o, y] = product
            centre_ref[2 + o, y] = response
            if y < 4:
                down_ref[o, y] = product
                down_ref[2 + o, y] = response
            if y >= 12:
                up_ref[o, y - 12] = product
                up_ref[2 + o, y - 12] = response


def swap_blocks(rows):
    block = lax.broadcasted_iota(jnp.int32, rows[0].shape, rows[0].ndim - 1) // 16
    for d in (1, 2, 4):
        keep = (block // d) % 2 == 0
        out = list(rows)
        for k in range(8):
            if k & d == 0:
                a, b = rows[k], rows[k + d]
                out[k] = jnp.where(keep, a, pltpu.roll(b, 16 * d, 1))
                out[k + d] = jnp.where(keep, pltpu.roll(a, 128 - 16 * d, 1), b)
        rows = out
    return rows


def second_kernel(
    centre_ref, lo_ref, hi_ref, below_ref, above_ref, scale_ref, orb_ref, occ_ref, zero_ref,
    resp_ref, out_ref, p_ref, u_ref, sc_ref, a_ref, b_ref, dens_ref,
):
    zero = zero_ref[0]
    for o in range(2):
        assemble(padded_row(centre_ref, lo_ref, hi_ref, o), above_ref, below_ref, o, p_ref, o)
        assemble(padded_row(centre_ref, lo_ref, hi_ref, 2 + o), above_ref, below_ref, 2 + o, u_ref, o)
    for o in range(2):
        sources(p_ref, scale_ref, sc_ref, o, zero)
        sweep(u_ref, scale_ref, sc_ref, o, zero, 1, into(a_ref, o, zero))
        sweep(a_ref, scale_ref, sc_ref, o, zero, 2, into(b_ref, o, zero))
        sweep(b_ref, scale_ref, sc_ref, o, zero, 3, into(a_ref, o, zero))
        last_sweep(a_ref, scale_ref, sc_ref, o, zero, orb_ref, occ_ref, resp_ref, dens_ref)
    for part in range(4):
        y, z = part // 2, 8 * (part % 2)
        blocks = swap_blocks([dens_ref[2 * k + y, z : z + 8] for k in range(8)])
        for b in range(8):
            out_ref[b, part] = blocks[b]


def final_kernel(own_ref, last_ref, resp_ref, dens_ref, response_ref):
    response_ref[...] = resp_ref[...]
    for part in range(4):
        y, z = part // 2, 8 * (part % 2)
        total = own_ref[part] + last_ref[part]
        for k in range(8):
            moved = total if k == 0 else pltpu.roll(total, 128 - 16 * k, 1)
            dens_ref[2 * k + y, z : z + 8, :] = moved[:, :16]


def ring(axis, step):
    count = lax.axis_size(axis)
    return [(i, (i + step) % count) for i in range(count)]


def exchange_y(up, down):
    return lax.ppermute(up, "gy", ring("gy", 1)), lax.ppermute(down, "gy", ring("gy", -1))


def exchange_z(centre, lo, hi):
    fields = centre.shape[0]
    strip = f32(fields, 12, 8, 128)
    tail, head = call(pack_kernel, (strip, strip), centre, lo, hi)
    return lax.ppermute(head, "gz", ring("gz", -1)), lax.ppermute(tail, "gz", ring("gz", 1))


def partner(value, *steps):
    count = lax.axis_size("bands")
    return lax.ppermute(value, "bands", [(i, i ^ steps[i % len(steps)]) for i in range(count)])


def on_device(orbitals, orbital_shift, occupation, potential, perturbation, kernel):
    group = lax.axis_index("bands")
    core, chip = group % 2, group // 2
    padded = f32(2, 24, 32, 128)
    wide = pltpu.VMEM((2, 24, 32, 128), jnp.float32)
    zero = jnp.zeros((1,), jnp.int32)

    def ends(field):
        return field[12:16], field[0:4]

    edges = lax.optimization_barrier([ends(field) for field in (perturbation, potential, orbitals[0], orbitals[1])])
    up, down = call(strips_kernel, (f32(3, 4, 16, 128), f32(3, 4, 16, 128)), *(end for pair in edges for end in pair))
    centre = jnp.concatenate([perturbation[None] * orbitals, potential[None]], 0)
    lo, hi = exchange_y(up, down)
    above, below = exchange_z(centre, lo, hi)
    response, partial, scale = call(
        first_kernel, (f32(2, 16, 16, 128), f32(16, 16, 128), padded),
        centre, lo, hi, below, above, orbitals, orbital_shift, occupation, zero,
        scratch=[wide] * 4, smem=3,
    )

    own = lax.dynamic_slice_in_dim(partial, 8 * core, 8, 0)
    own = own + partner(lax.dynamic_slice_in_dim(partial, 8 * (1 - core), 8, 0), 1)
    own = own + partner(own, 6, 2)
    own = own + partner(own, 2, 6)
    other = partner(own, 1)
    centre, up, down = call(
        change_kernel, (f32(4, 16, 16, 128), f32(4, 4, 16, 128), f32(4, 4, 16, 128)),
        own, other, perturbation, kernel, orbitals, response, core[None].astype(jnp.int32), smem=1,
    )
    lo, hi = exchange_y(up, down)
    above, below = exchange_z(centre, lo, hi)
    response, blocks = call(
        second_kernel, (f32(2, 16, 16, 128), f32(8, 4, 8, 128)),
        centre, lo, hi, below, above, scale, orbitals, occupation, zero,
        scratch=[wide] * 5 + [pltpu.VMEM((16, 16, 128), jnp.float32)], smem=2,
    )

    blocks = blocks.reshape(4, 2, 4, 8, 128)
    kept = lax.dynamic_index_in_dim(blocks, core, 1, keepdims=False)
    kept = kept + partner(lax.dynamic_index_in_dim(blocks, 1 - core, 1, keepdims=False), 1)

    def block_of(step):
        return lax.dynamic_index_in_dim(kept, chip ^ step, 0, keepdims=False)

    first, second = 3 - 2 * core, 1 + 2 * core
    pair = jnp.stack([block_of(0), block_of(second)]) + partner(jnp.stack([block_of(first), block_of(2)]), 6, 2)
    last = partner(pair[1], 2, 6)
    density, response = call(
        final_kernel, (f32(16, 16, 16), f32(2, 16, 16, 128)), pair[0], last, response
    )
    return response, density


def solution(mesh):
    placed = (
        P("bands", "gy", "gz", None),
        P("bands"),
        P("bands"),
        P("gy", "gz", None),
        P("gy", "gz", None),
        P("gy", "gz", None),
    )
    return jax.shard_map(
        on_device,
        mesh=mesh,
        in_specs=placed,
        out_specs=(P("bands", "gy", "gz", None), P("gy", "gz", "bands")),
        check_vma=False,
    )
```

```python
import functools

import jax
import jax.numpy as jnp
from jax import lax
from jax.experimental import pallas as pl
from jax.experimental.pallas import tpu as pltpu
from jax.sharding import PartitionSpec as P

RELAX = 0.8
HALO = 4
VMEM = pl.BlockSpec(memory_space=pltpu.VMEM)
SMEM = pl.BlockSpec(memory_space=pltpu.SMEM)


def call(body, outs, *args, scratch=(), smem=0):
    return pl.pallas_call(
        body,
        out_shape=outs,
        in_specs=[VMEM] * (len(args) - smem) + [SMEM] * smem,
        out_specs=jax.tree.map(lambda _: VMEM, outs),
        scratch_shapes=list(scratch),
        compiler_params=pltpu.CompilerParams(vmem_limit_bytes=48 * 2**20),
    )(*args)


def f32(*shape):
    return jax.ShapeDtypeStruct(shape, jnp.float32)


def low_half():
    return lax.broadcasted_iota(jnp.int32, (8, 128), 0) < 4


def pack_z(row, head_ref, tail_ref, field):
    low = low_half()
    for j in range(12):
        a, b = row(j), row(j + 12)
        head_ref[field, j] = jnp.where(low, a[:8], pltpu.roll(b[:8], 4, 0))
        tail_ref[field, j] = jnp.where(low, pltpu.roll(b[8:], 4, 0), a[8:])


def padded_row(centre_ref, lo_ref, hi_ref, field):
    def row(r):
        if r < 4:
            return lo_ref[field, r]
        if r < 20:
            return centre_ref[field, r - 4]
        return hi_ref[field, r - 20]

    return row


def pack_kernel(extras, centre_ref, lo_ref, hi_ref, *refs):
    tail_ref, head_ref = refs[extras : extras + 2]
    for source_ref, dest_ref in zip(refs[:extras], refs[extras + 2 :]):
        dest_ref[...] = source_ref[...]
    for field in range(centre_ref.shape[0]):
        pack_z(padded_row(centre_ref, lo_ref, hi_ref, field), head_ref, tail_ref, field)


def assemble(row, above_ref, below_ref, field, dest_ref, at):
    for r in range(24):
        dest_ref[at, r, 8:24] = row(r)
    for j in range(12):
        above, below = above_ref[field, j], below_ref[field, j]
        dest_ref[at, j, 24:32] = above
        dest_ref[at, j, 0:8] = below
        dest_ref[at, j + 12, 24:32] = pltpu.roll(above, 4, 0)
        dest_ref[at, j + 12, 0:8] = pltpu.roll(below, 4, 0)


def window(zero, last=False):
    first, count = (8, 16) if last else (4, 24)
    return [pl.ds(zero + first + k, count) for k in (0, -1, 1)]


def shifts_x(u):
    return pltpu.roll(u, 1, u.ndim - 1) + pltpu.roll(u, 127, u.ndim - 1)


def by_rows(first, last, load, emit):
    before, at = load(first - 1), load(first)
    for r in range(first, last):
        after = load(r + 1)
        emit(r, before, at, after)
        before, at = at, after


def sources(p_ref, scale_ref, sc_ref, o, zero):
    here, down, up = window(zero)

    def load(r):
        return p_ref[o, r, here]

    def emit(r, before, at, after):
        faces = shifts_x(at) + (p_ref[o, r, down] + p_ref[o, r, up]) + (before + after)
        sc_ref[o, r, here] = scale_ref[o, r, here] * (-30.0 * at - 5.0 * faces)

    by_rows(1, 23, load, emit)


def sweep(src_ref, scale_ref, sc_ref, o, zero, margin, store):
    here, down, up = window(zero, margin == 4)

    def load(r):
        return src_ref[o, r, here], src_ref[o, r, down] + src_ref[o, r, up]

    def emit(r, before, at, after):
        u, along_z = at
        across = before[1] + after[1]
        m = before[0] + after[0] + along_z
        n = 3.0 * m + across
        total = shifts_x(14.0 * u + n) + (3.0 * n + 5.0 * m)
        store(r, 0.2 * u + sc_ref[o, r, here] + scale_ref[o, r, here] * total)

    by_rows(margin, 24 - margin, load, emit)


def into(dest_ref, o, zero):
    here = window(zero)[0]

    def store(r, new):
        dest_ref[o, r, here] = new

    return store


def last_sweep(src_ref, scale_ref, sc_ref, o, zero, orb_ref, occ_ref, resp_ref, dens_ref):
    occupation = jnp.concatenate([occ_ref[o]] * 2, 0)

    def store(r, new):
        resp_ref[o, r - 4] = new
        term = occupation * orb_ref[o, r - 4] * new
        dens_ref[r - 4] = term if o == 0 else dens_ref[r - 4] + term

    sweep(src_ref, scale_ref, sc_ref, o, zero, 4, store)


def first_kernel(
    centre_ref, lo_ref, hi_ref, below_ref, above_ref, orb_ref, shift_ref, occ_ref, zero_ref,
    resp_ref, dens_ref, scale_ref, p_ref, sc_ref, a_ref, b_ref,
):
    zero = zero_ref[0]
    for field in range(2):
        assemble(padded_row(centre_ref, lo_ref, hi_ref, field), above_ref, below_ref, field, p_ref, field)
    assemble(padded_row(centre_ref, lo_ref, hi_ref, 2), above_ref, below_ref, 2, a_ref, 0)
    for o in range(2):
        base = 32.0 / 15.0 + jnp.concatenate([shift_ref[o]] * 4, 0)

        for r in range(1, 23):
            scale_ref[o, r, 0:32] = (RELAX / 60.0) / (base + a_ref[0, r, 0:32])
    for o in range(2):
        sources(p_ref, scale_ref, sc_ref, o, zero)
    for o in range(2):
        sweep(sc_ref, scale_ref, sc_ref, o, zero, 2, into(a_ref, o, zero))
        sweep(a_ref, scale_ref, sc_ref, o, zero, 3, into(b_ref, o, zero))
        last_sweep(b_ref, scale_ref, sc_ref, o, zero, orb_ref, occ_ref, resp_ref, dens_ref)


def strips_kernel(*refs):
    perturbation, potential, orbitals, dests = refs[0:2], refs[2:4], (refs[4:6], refs[6:8]), refs[8:10]
    for end, dest_ref in enumerate(dests):
        for y in range(4):
            for o in range(2):
                dest_ref[o, y] = perturbation[end][y] * orbitals[o][end][y]
            dest_ref[2, y] = potential[end][y]


def change_kernel(own_ref, other_ref, pert_ref, kern_ref, orb_ref, resp_ref, core_ref, centre_ref, up_ref, down_ref):
    first_core = core_ref[0] == 0
    for y in range(16):
        mine, theirs = own_ref[y % 8], other_ref[y % 8]
        total = jnp.where(first_core, mine, theirs) if y < 8 else jnp.where(first_core, theirs, mine)
        change = pert_ref[y] + kern_ref[y] * total
        for o in range(2):
            product, response = change * orb_ref[o, y], resp_ref[o, y]
            centre_ref[o, y] = product
            centre_ref[2 + o, y] = response
            if y < 4:
                down_ref[o, y] = product
                down_ref[2 + o, y] = response
            if y >= 12:
                up_ref[o, y - 12] = product
                up_ref[2 + o, y - 12] = response


def swap_blocks(rows):
    block = lax.broadcasted_iota(jnp.int32, rows[0].shape, rows[0].ndim - 1) // 16
    for d in (1, 2, 4):
        keep = (block // d) % 2 == 0
        out = list(rows)
        for k in range(8):
            if k & d == 0:
                a, b = rows[k], rows[k + d]
                out[k] = jnp.where(keep, a, pltpu.roll(b, 16 * d, 1))
                out[k + d] = jnp.where(keep, pltpu.roll(a, 128 - 16 * d, 1), b)
        rows = out
    return rows


def second_kernel(
    centre_ref, lo_ref, hi_ref, below_ref, above_ref, scale_ref, orb_ref, occ_ref, zero_ref,
    resp_ref, out_ref, p_ref, u_ref, sc_ref, a_ref, b_ref, dens_ref,
):
    zero = zero_ref[0]
    for o in range(2):
        assemble(padded_row(centre_ref, lo_ref, hi_ref, o), above_ref, below_ref, o, p_ref, o)
        assemble(padded_row(centre_ref, lo_ref, hi_ref, 2 + o), above_ref, below_ref, 2 + o, u_ref, o)
    for o in range(2):
        sources(p_ref, scale_ref, sc_ref, o, zero)
        sweep(u_ref, scale_ref, sc_ref, o, zero, 1, into(a_ref, o, zero))
        sweep(a_ref, scale_ref, sc_ref, o, zero, 2, into(b_ref, o, zero))
        sweep(b_ref, scale_ref, sc_ref, o, zero, 3, into(a_ref, o, zero))
        last_sweep(a_ref, scale_ref, sc_ref, o, zero, orb_ref, occ_ref, resp_ref, dens_ref)
    for part in range(4):
        y, z = part // 2, 8 * (part % 2)
        blocks = swap_blocks([dens_ref[2 * k + y, z : z + 8] for k in range(8)])
        for b in range(8):
            out_ref[b, part] = blocks[b]


def final_kernel(own_ref, last_ref, resp_ref, dens_ref, response_ref):
    response_ref[...] = resp_ref[...]
    for part in range(4):
        y, z = part // 2, 8 * (part % 2)
        total = own_ref[part] + last_ref[part]
        for k in range(8):
            moved = total if k == 0 else pltpu.roll(total, 128 - 16 * k, 1)
            dens_ref[2 * k + y, z : z + 8, :] = moved[:, :16]


def ring(axis, step):
    count = lax.axis_size(axis)
    return [(i, (i + step) % count) for i in range(count)]


def exchange_y(up, down):
    return lax.ppermute(up, "gy", ring("gy", 1)), lax.ppermute(down, "gy", ring("gy", -1))


def exchange_z(centre, lo, hi, *extras):
    fields = centre.shape[0]
    strip = f32(fields, 12, 8, 128)
    tail, head, *extras = call(
        functools.partial(pack_kernel, len(extras)), (strip, strip, *(f32(*each.shape) for each in extras)), centre, lo, hi, *extras
    )
    return lax.ppermute(head, "gz", ring("gz", -1)), lax.ppermute(tail, "gz", ring("gz", 1)), *extras


def partner(value, *steps):
    count = lax.axis_size("bands")
    return lax.ppermute(value, "bands", [(i, i ^ steps[i % len(steps)]) for i in range(count)])


def on_device(orbitals, orbital_shift, occupation, potential, perturbation, kernel):
    group = lax.axis_index("bands")
    core, chip = group % 2, group // 2
    padded = f32(2, 24, 32, 128)
    wide = pltpu.VMEM((2, 24, 32, 128), jnp.float32)
    zero = (lax.axis_index("gz") // 64)[None].astype(jnp.int32)
    shifts, occupations = (jnp.broadcast_to(each[:, None, None], (2, 8, 128)) for each in (orbital_shift, occupation))

    def ends(field):
        return field[12:16], field[0:4]

    edges = lax.optimization_barrier([ends(field) for field in (perturbation, potential, orbitals[0], orbitals[1])])
    up, down = call(strips_kernel, (f32(3, 4, 16, 128), f32(3, 4, 16, 128)), *(end for pair in edges for end in pair))
    centre = jnp.concatenate([perturbation[None] * orbitals, potential[None]], 0)
    lo, hi = exchange_y(up, down)
    above, below, shifts, occupations = exchange_z(centre, lo, hi, shifts, occupations)
    response, partial, scale = call(
        first_kernel, (f32(2, 16, 16, 128), f32(16, 16, 128), padded),
        centre, lo, hi, below, above, orbitals, shifts, occupations, zero,
        scratch=[wide] * 4, smem=1,
    )

    own = lax.dynamic_slice_in_dim(partial, 8 * core, 8, 0)
    own = own + partner(lax.dynamic_slice_in_dim(partial, 8 * (1 - core), 8, 0), 1)
    own = own + partner(own, 6, 2)
    own = own + partner(own, 2, 6)
    other = partner(own, 1)
    centre, up, down = call(
        change_kernel, (f32(4, 16, 16, 128), f32(4, 4, 16, 128), f32(4, 4, 16, 128)),
        own, other, perturbation, kernel, orbitals, response, core[None].astype(jnp.int32), smem=1,
    )
    lo, hi = exchange_y(up, down)
    above, below = exchange_z(centre, lo, hi)
    response, blocks = call(
        second_kernel, (f32(2, 16, 16, 128), f32(8, 4, 8, 128)),
        centre, lo, hi, below, above, scale, orbitals, occupations, zero,
        scratch=[wide] * 5 + [pltpu.VMEM((16, 16, 128), jnp.float32)], smem=1,
    )

    blocks = blocks.reshape(4, 2, 4, 8, 128)
    kept = lax.dynamic_index_in_dim(blocks, core, 1, keepdims=False)
    kept = kept + partner(lax.dynamic_index_in_dim(blocks, 1 - core, 1, keepdims=False), 1)

    def block_of(step):
        return lax.dynamic_index_in_dim(kept, chip ^ step, 0, keepdims=False)

    first, second = 3 - 2 * core, 1 + 2 * core
    pair = jnp.stack([block_of(0), block_of(second)]) + partner(jnp.stack([block_of(first), block_of(2)]), 6, 2)
    last = partner(pair[1], 2, 6)
    density, response = call(
        final_kernel, (f32(16, 16, 16), f32(2, 16, 16, 128)), pair[0], last, response
    )
    return response, density


def solution(mesh):
    placed = (
        P("bands", "gy", "gz", None),
        P("bands"),
        P("bands"),
        P("gy", "gz", None),
        P("gy", "gz", None),
        P("gy", "gz", None),
    )
    return jax.shard_map(
        on_device,
        mesh=mesh,
        in_specs=placed,
        out_specs=(P("bands", "gy", "gz", None), P("gy", "gz", "bands")),
        check_vma=False,
    )
```

```python
import functools

import jax
import jax.numpy as jnp
from jax import lax
from jax.experimental import pallas as pl
from jax.experimental.pallas import tpu as pltpu
from jax.sharding import PartitionSpec as P

RELAX = 0.8
HALO = 4
VMEM = pl.BlockSpec(memory_space=pltpu.VMEM)
SMEM = pl.BlockSpec(memory_space=pltpu.SMEM)


def call(body, outs, *args, scratch=(), smem=0):
    return pl.pallas_call(
        body,
        out_shape=outs,
        in_specs=[VMEM] * (len(args) - smem) + [SMEM] * smem,
        out_specs=jax.tree.map(lambda _: VMEM, outs),
        scratch_shapes=list(scratch),
        compiler_params=pltpu.CompilerParams(vmem_limit_bytes=48 * 2**20),
    )(*args)


def f32(*shape):
    return jax.ShapeDtypeStruct(shape, jnp.float32)


def low_half():
    return lax.broadcasted_iota(jnp.int32, (8, 128), 0) < 4


def pack_z(row, head_ref, tail_ref, field):
    low = low_half()
    for j in range(12):
        a, b = row(j), row(j + 12)
        head_ref[field, j] = jnp.where(low, a[:8], pltpu.roll(b[:8], 4, 0))
        tail_ref[field, j] = jnp.where(low, pltpu.roll(b[8:], 4, 0), a[8:])


def padded_row(centre_ref, lo_ref, hi_ref, field):
    def row(r):
        if r < 4:
            return lo_ref[field, r]
        if r < 20:
            return centre_ref[field, r - 4]
        return hi_ref[field, r - 20]

    return row


def pack_kernel(extras, centre_ref, lo_ref, hi_ref, *refs):
    tail_ref, head_ref = refs[extras : extras + 2]
    for source_ref, dest_ref in zip(refs[:extras], refs[extras + 2 :]):
        dest_ref[...] = source_ref[...]
    for field in range(centre_ref.shape[0]):
        pack_z(padded_row(centre_ref, lo_ref, hi_ref, field), head_ref, tail_ref, field)


def assemble(row, above_ref, below_ref, field, dest_ref, at):
    for r in range(24):
        dest_ref[at, r, 8:24] = row(r)
    for j in range(12):
        above, below = above_ref[field, j], below_ref[field, j]
        dest_ref[at, j, 24:32] = above
        dest_ref[at, j, 0:8] = below
        dest_ref[at, j + 12, 24:32] = pltpu.roll(above, 4, 0)
        dest_ref[at, j + 12, 0:8] = pltpu.roll(below, 4, 0)


def window(zero, last=False):
    first, count = (8, 16) if last else (4, 24)
    return [pl.ds(zero + first + k, count) for k in (0, -1, 1)]


def shifts_x(u):
    return pltpu.roll(u, 1, u.ndim - 1) + pltpu.roll(u, 127, u.ndim - 1)


def by_rows(first, last, load, emit):
    before, at = load(first - 1), load(first)
    for r in range(first, last):
        after = load(r + 1)
        emit(r, before, at, after)
        before, at = at, after


def sources(p_ref, scale_ref, sc_ref, o, zero):
    here, down, up = window(zero)

    def load(r):
        return p_ref[o, r, here]

    def emit(r, before, at, after):
        faces = shifts_x(at) + (p_ref[o, r, down] + p_ref[o, r, up]) + (before + after)
        sc_ref[o, r, here] = scale_ref[o, r, here] * (-30.0 * at - 5.0 * faces)

    by_rows(1, 23, load, emit)


def sweep(src_ref, scale_ref, sc_ref, o, zero, margin, store):
    here, down, up = window(zero, margin == 4)

    def load(r):
        return src_ref[o, r, here], src_ref[o, r, down] + src_ref[o, r, up]

    def emit(r, before, at, after):
        u, along_z = at
        across = before[1] + after[1]
        m = before[0] + after[0] + along_z
        n = 3.0 * m + across
        total = shifts_x(14.0 * u + n) + (3.0 * n + 5.0 * m)
        store(r, 0.2 * u + sc_ref[o, r, here] + scale_ref[o, r, here] * total)

    by_rows(margin, 24 - margin, load, emit)


def into(dest_ref, o, zero):
    here = window(zero)[0]

    def store(r, new):
        dest_ref[o, r, here] = new

    return store


def last_sweep(src_ref, scale_ref, sc_ref, o, zero, orb_ref, occ_ref, resp_ref, dens_ref):
    occupation = jnp.concatenate([occ_ref[o]] * 2, 0)

    def store(r, new):
        resp_ref[o, r - 4] = new
        term = occupation * orb_ref[o, r - 4] * new
        dens_ref[r - 4] = term if o == 0 else dens_ref[r - 4] + term

    sweep(src_ref, scale_ref, sc_ref, o, zero, 4, store)


def first_kernel(
    centre_ref, lo_ref, hi_ref, below_ref, above_ref, orb_ref, shift_ref, occ_ref, zero_ref,
    resp_ref, dens_ref, scale_ref, p_ref, sc_ref, a_ref, b_ref,
):
    zero = zero_ref[0]
    for field in range(2):
        assemble(padded_row(centre_ref, lo_ref, hi_ref, field), above_ref, below_ref, field, p_ref, field)
    assemble(padded_row(centre_ref, lo_ref, hi_ref, 2), above_ref, below_ref, 2, a_ref, 0)
    for o in range(2):
        base = 32.0 / 15.0 + jnp.concatenate([shift_ref[o]] * 4, 0)

        for r in range(1, 23):
            scale_ref[o, r, 0:32] = (RELAX / 60.0) / (base + a_ref[0, r, 0:32])
    for o in range(2):
        sources(p_ref, scale_ref, sc_ref, o, zero)
    for o in range(2):
        sweep(sc_ref, scale_ref, sc_ref, o, zero, 2, into(a_ref, o, zero))
        sweep(a_ref, scale_ref, sc_ref, o, zero, 3, into(b_ref, o, zero))
        last_sweep(b_ref, scale_ref, sc_ref, o, zero, orb_ref, occ_ref, resp_ref, dens_ref)


def strips_kernel(*refs):
    perturbation, potential, orbitals, dests = refs[0:2], refs[2:4], (refs[4:6], refs[6:8]), refs[8:10]
    for end, dest_ref in enumerate(dests):
        for y in range(4):
            for o in range(2):
                dest_ref[o, y] = perturbation[end][y] * orbitals[o][end][y]
            dest_ref[2, y] = potential[end][y]


def change_kernel(own_ref, other_ref, pert_ref, kern_ref, orb_ref, resp_ref, core_ref, centre_ref, up_ref, down_ref):
    first_core = core_ref[0] == 0
    for y in range(16):
        mine, theirs = own_ref[y % 8], other_ref[y % 8]
        total = jnp.where(first_core, mine, theirs) if y < 8 else jnp.where(first_core, theirs, mine)
        change = pert_ref[y] + kern_ref[y] * total
        for o in range(2):
            product, response = change * orb_ref[o, y], resp_ref[o, y]
            centre_ref[o, y] = product
            centre_ref[2 + o, y] = response
            if y < 4:
                down_ref[o, y] = product
                down_ref[2 + o, y] = response
            if y >= 12:
                up_ref[o, y - 12] = product
                up_ref[2 + o, y - 12] = response


def swap_blocks(rows):
    block = lax.broadcasted_iota(jnp.int32, rows[0].shape, rows[0].ndim - 1) // 16
    for d in (1, 2, 4):
        keep = (block // d) % 2 == 0
        out = list(rows)
        for k in range(8):
            if k & d == 0:
                a, b = rows[k], rows[k + d]
                out[k] = jnp.where(keep, a, pltpu.roll(b, 16 * d, 1))
                out[k + d] = jnp.where(keep, pltpu.roll(a, 128 - 16 * d, 1), b)
        rows = out
    return rows


def second_kernel(
    centre_ref, lo_ref, hi_ref, below_ref, above_ref, scale_ref, orb_ref, occ_ref, zero_ref,
    resp_ref, out_ref, p_ref, u_ref, sc_ref, a_ref, b_ref, dens_ref,
):
    zero = zero_ref[0]
    for o in range(2):
        assemble(padded_row(centre_ref, lo_ref, hi_ref, o), above_ref, below_ref, o, p_ref, o)
        assemble(padded_row(centre_ref, lo_ref, hi_ref, 2 + o), above_ref, below_ref, 2 + o, u_ref, o)
    for o in range(2):
        sources(p_ref, scale_ref, sc_ref, o, zero)
        sweep(u_ref, scale_ref, sc_ref, o, zero, 1, into(a_ref, o, zero))
        sweep(a_ref, scale_ref, sc_ref, o, zero, 2, into(b_ref, o, zero))
        sweep(b_ref, scale_ref, sc_ref, o, zero, 3, into(a_ref, o, zero))
        last_sweep(a_ref, scale_ref, sc_ref, o, zero, orb_ref, occ_ref, resp_ref, dens_ref)
    for part in range(4):
        y, z = part // 2, 8 * (part % 2)
        blocks = swap_blocks([dens_ref[2 * k + y, z : z + 8] for k in range(8)])
        for b in range(8):
            out_ref[b, part] = blocks[b]


def final_kernel(own_ref, one_ref, two_ref, three_ref, resp_ref, dens_ref, response_ref):
    response_ref[...] = resp_ref[...]
    for part in range(4):
        y, z = part // 2, 8 * (part % 2)
        total = (own_ref[part] + one_ref[part]) + (two_ref[part] + three_ref[part])
        for k in range(8):
            moved = total if k == 0 else pltpu.roll(total, 128 - 16 * k, 1)
            dens_ref[2 * k + y, z : z + 8, :] = moved[:, :16]


def ring(axis, step):
    count = lax.axis_size(axis)
    return [(i, (i + step) % count) for i in range(count)]


def exchange_y(up, down):
    return lax.ppermute(up, "gy", ring("gy", 1)), lax.ppermute(down, "gy", ring("gy", -1))


def exchange_z(centre, lo, hi, *extras):
    fields = centre.shape[0]
    strip = f32(fields, 12, 8, 128)
    tail, head, *extras = call(
        functools.partial(pack_kernel, len(extras)), (strip, strip, *(f32(*each.shape) for each in extras)), centre, lo, hi, *extras
    )
    return lax.ppermute(head, "gz", ring("gz", -1)), lax.ppermute(tail, "gz", ring("gz", 1)), *extras


def partner(value, *steps):
    count = lax.axis_size("bands")
    return lax.ppermute(value, "bands", [(i, i ^ steps[i % len(steps)]) for i in range(count)])


def on_device(orbitals, orbital_shift, occupation, potential, perturbation, kernel):
    group = lax.axis_index("bands")
    core, chip = group % 2, group // 2
    padded = f32(2, 24, 32, 128)
    wide = pltpu.VMEM((2, 24, 32, 128), jnp.float32)
    zero = (lax.axis_index("gz") // 64)[None].astype(jnp.int32)
    shifts, occupations = (jnp.broadcast_to(each[:, None, None], (2, 8, 128)) for each in (orbital_shift, occupation))

    def ends(field):
        return field[12:16], field[0:4]

    edges = lax.optimization_barrier([ends(field) for field in (perturbation, potential, orbitals[0], orbitals[1])])
    up, down = call(strips_kernel, (f32(3, 4, 16, 128), f32(3, 4, 16, 128)), *(end for pair in edges for end in pair))
    centre = jnp.concatenate([perturbation[None] * orbitals, potential[None]], 0)
    lo, hi = exchange_y(up, down)
    above, below, shifts, occupations = exchange_z(centre, lo, hi, shifts, occupations)
    response, partial, scale = call(
        first_kernel, (f32(2, 16, 16, 128), f32(16, 16, 128), padded),
        centre, lo, hi, below, above, orbitals, shifts, occupations, zero,
        scratch=[wide] * 4, smem=1,
    )

    own = lax.dynamic_slice_in_dim(partial, 8 * core, 8, 0)
    own = own + partner(lax.dynamic_slice_in_dim(partial, 8 * (1 - core), 8, 0), 1)
    own = own + partner(own, 6, 2)
    own = own + partner(own, 2, 6)
    other = partner(own, 1)
    centre, up, down = call(
        change_kernel, (f32(4, 16, 16, 128), f32(4, 4, 16, 128), f32(4, 4, 16, 128)),
        own, other, perturbation, kernel, orbitals, response, core[None].astype(jnp.int32), smem=1,
    )
    lo, hi = exchange_y(up, down)
    above, below = exchange_z(centre, lo, hi)
    response, blocks = call(
        second_kernel, (f32(2, 16, 16, 128), f32(8, 4, 8, 128)),
        centre, lo, hi, below, above, scale, orbitals, occupations, zero,
        scratch=[wide] * 5 + [pltpu.VMEM((16, 16, 128), jnp.float32)], smem=1,
    )

    blocks = blocks.reshape(4, 2, 4, 8, 128)
    kept = lax.dynamic_index_in_dim(blocks, core, 1, keepdims=False)
    kept = kept + partner(lax.dynamic_index_in_dim(blocks, 1 - core, 1, keepdims=False), 1)

    def block_of(step):
        return lax.dynamic_index_in_dim(kept, chip ^ step, 0, keepdims=False)

    two, one, three = (partner(block_of(step), 2 * step) for step in (2, 1, 3))
    density, response = call(
        final_kernel, (f32(16, 16, 16), f32(2, 16, 16, 128)), block_of(0), one, two, three, response
    )
    return response, density


def solution(mesh):
    placed = (
        P("bands", "gy", "gz", None),
        P("bands"),
        P("bands"),
        P("gy", "gz", None),
        P("gy", "gz", None),
        P("gy", "gz", None),
    )
    return jax.shard_map(
        on_device,
        mesh=mesh,
        in_specs=placed,
        out_specs=(P("bands", "gy", "gz", None), P("gy", "gz", "bands")),
        check_vma=False,
    )
```
